512 devices in a mesh: tile: 128 (over z, y, core), cam: 4 (over x).
Axes of the slice: x: 4, y: 8, z: 8, core: 2. Of those that a mesh axis runs over, the one named last changes fastest.
Arguments:
- gaussians: float32 [59, 65536], P(None, 'tile')
- moment_one: float32 [59, 65536], P(None, 'tile'), may hold values from -3 to 3
- moment_two: float32 [59, 65536], P(None, 'tile'), may hold values from 0.01 to 1
- cameras: float32 [4, 4], P('cam')
- requests: int32 [4, 131072], P('cam', 'tile'), may hold values from 0 to 511
- tile_lists: int32 [4, 128, 1024], P('cam', 'tile'), may hold values from 0 to 1023
- tile_lengths: int32 [4, 128], P('cam', 'tile'), may hold values from 1 to 1024, as said below
- cotangent: float32 [4, 128, 3, 256], P('cam', 'tile'), may hold values from -6 to 6
Outputs:
- gradient: float32 [59, 65536], P(None, 'tile')
- updated: float32 [59, 65536], P(None, 'tile')
- first_new: float32 [59, 65536], P(None, 'tile')
- second_new: float32 [59, 65536], P(None, 'tile')
The draws below stay inside these ranges and needn't reach their ends.
Inputs may be any that keep to these rules, and one draw needn't show every extreme that they name: `requests`: each device asks every owner, for each camera, for exactly 8 rows by local index; a row may be asked more than once. `tile_lists`: slot o * 8 + s names the s-th row fetched from owner o by the device holding the tile. `tile_lengths`: slots from the length on are unused; some tile of every draw is full.
All inputs are finite; a program needn't handle non-finite values.
Results may differ from the reference program's by a relative error of at most 0.0003.
Values sent between devices are 32-bit elements; how exact they have to be, the bound alone decides.
A program may use at most 64 MiB of HBM per device.

```python
import math
import jax
import jax.numpy as jnp
from jax import lax

PARAMS = 59
TILE_PIX = 256
IMG_TILES = 16
TILES_DEV = 1
CAP = 8
G_DEV = 512
CAMERAS = 4
TILES = 128
G = 65536
SLOTS = 1024
MAXL = 1024
N_TILE = 128


def draw_gaussians(key, part):
    key = jax.random.fold_in(key, 1)
    keys = jax.random.split(key, 8)
    means_x = jax.random.uniform(keys[0], (1, G), jnp.float32, -1.0, 1.0)
    depth = jax.random.uniform(keys[1], (1, G), jnp.float32, 4.0, 6.0)
    height_unit = jax.random.uniform(keys[7], (1, G), jnp.float32, -1.0, 1.0)
    means_y = height_unit * depth * (8.0 * TILES / IMG_TILES / 350.0)
    log_scales = jax.random.uniform(keys[2], (3, G), jnp.float32, -1.2, -0.2)
    quat_w = jax.random.uniform(keys[3], (1, G), jnp.float32, 1.0, 2.0)
    quat_v = jax.random.uniform(keys[4], (3, G), jnp.float32, -0.5, 0.5)
    logits = jax.random.uniform(keys[5], (1, G), jnp.float32, -7.0, -3.0)
    colour = 0.3 * jax.random.normal(keys[6], (48, G), jnp.float32)
    return jnp.concatenate([means_x, means_y, depth, log_scales, quat_w, quat_v, logits, colour], axis=0)


def draw_cameras(key, part):
    key = jax.random.fold_in(key, 2)
    keys = jax.random.split(key, 2)
    anchor = jax.random.uniform(keys[0], (CAMERAS, 3), jnp.float32, -0.3, 0.3)
    heading = jax.random.uniform(keys[1], (CAMERAS, 1), jnp.float32, -0.15, 0.15)
    return jnp.concatenate([anchor, heading], axis=1)


def draw_tile_lengths(key, part):
    key = jax.random.fold_in(key, 3)
    keys = jax.random.split(key, 2)
    short = jax.random.randint(keys[0], (CAMERAS, TILES), 1, MAXL // 3 + 1)
    full_pick = jax.random.randint(keys[1], (CAMERAS, TILES), 0, 10) == 0
    lengths = jnp.where(full_pick, MAXL, short).astype(jnp.int32)
    return lengths.at[0, 0].set(MAXL)


def place_ends(result, rng, smallest, high):
    extent = result.shape
    place = [jax.random.randint(jax.random.fold_in(rng, axis), (), 0, extent[axis]) for axis in range(len(extent))]
    result = result.at[tuple(place)].set(smallest)
    longest = extent.index(max(extent))
    place[longest] = (place[longest] + 1) % extent[longest]
    return result.at[tuple(place)].set(high)


def levels(stream_key, dims, cuts, smallest, top_value):
    factor_of = 1.0
    for axis_at, blocks in cuts:
        draws = jax.random.uniform(jax.random.fold_in(jax.random.fold_in(stream_key, 6), axis_at), (blocks,), jnp.float32, smallest / len(cuts), top_value / len(cuts))
        factor_of = factor_of * jnp.repeat(jnp.exp(draws), dims[axis_at] // blocks).reshape((-1,) + (1,) * (len(dims) - 1 - axis_at))
    return factor_of


def bell_draw(rng, extent, deviation, bound, cuts=(), kind=jnp.bfloat16):
    values = deviation * jax.random.normal(rng, extent, jnp.float32)
    if cuts:
        values = values * levels(rng, extent, cuts, -0.22, 0.18)
    return jnp.clip(values, -bound, bound).astype(kind)


def setup_inputs(seed: int = 0) -> dict:
    key_list = jax.random.split(jax.random.key(seed), 9)
    gaussians = draw_gaussians(jax.random.fold_in(key_list[8], 71), 0)
    moment_one = bell_draw(key_list[1], (PARAMS, G), 0.5, 3.0, ((1, 128),), jnp.float32)
    moment_two = jnp.clip(jnp.exp(math.log(1.0) - 4.6051702 * jax.random.uniform(key_list[2], (PARAMS, G), jnp.float32) ** levels(key_list[2], (PARAMS, G), ((1, 128),), -0.2, 0.2)), 0.01, 1.0)
    cameras = draw_cameras(jax.random.fold_in(key_list[8], 71), 0)
    requests = place_ends(jax.random.randint(key_list[4], (CAMERAS, N_TILE * SLOTS), 0, G_DEV), jax.random.fold_in(key_list[4], 1), 0, G_DEV - 1).astype(jnp.int32)
    tile_lists = place_ends(jax.random.randint(key_list[5], (CAMERAS, TILES, MAXL), 0, SLOTS), jax.random.fold_in(key_list[5], 1), 0, SLOTS - 1).astype(jnp.int32)
    tile_lengths = draw_tile_lengths(jax.random.fold_in(key_list[8], 71), 0)
    cotangent = bell_draw(key_list[7], (CAMERAS, TILES, 3, TILE_PIX), 1.0, 6.0, ((0, 4), (1, 128)), jnp.float32)
    return {"gaussians": gaussians, "moment_one": moment_one, "moment_two": moment_two, "cameras": cameras, "requests": requests, "tile_lists": tile_lists, "tile_lengths": tile_lengths, "cotangent": cotangent}


focal_length = 350.0
dilation = 0.3
tile_side = 16
sh_zero = 0.28209479177387814
sh_one = 0.4886025119029199
sh_two = [1.0925484305920792, -1.0925484305920792, 0.31539156525252005, -1.0925484305920792, 0.5462742152960396]
sh_three = [-0.5900435899266435, 2.890611442640554, -0.4570457994644658, 0.3731763325901154, -0.4570457994644658, 1.445305721320277, -0.5900435899266435]

def harmonics(dir_x, dir_y, dir_z):
    xx = dir_x * dir_x
    yy = dir_y * dir_y
    zz = dir_z * dir_z
    return [sh_zero + 0.0 * dir_x, -sh_one * dir_y, sh_one * dir_z, -sh_one * dir_x, sh_two[0] * dir_x * dir_y, sh_two[1] * dir_y * dir_z, sh_two[2] * (2.0 * zz - xx - yy), sh_two[3] * dir_x * dir_z, sh_two[4] * (xx - yy), sh_three[0] * dir_y * (3.0 * xx - yy), sh_three[1] * dir_x * dir_y * dir_z, sh_three[2] * dir_y * (4.0 * zz - xx - yy), sh_three[3] * dir_z * (2.0 * zz - 3.0 * xx - 3.0 * yy), sh_three[4] * dir_x * (4.0 * zz - xx - yy), sh_three[5] * dir_z * (xx - yy), sh_three[6] * dir_x * (xx - 3.0 * yy)]

def screen_of(rows, camera, centre_y):
    rel_x = rows[0] - camera[0]
    rel_y = rows[1] - camera[1]
    rel_z = rows[2] - camera[2]
    cos_yaw = jnp.cos(camera[3])
    sin_yaw = jnp.sin(camera[3])
    view = [[cos_yaw, 0.0, -sin_yaw], [0.0, 1.0, 0.0], [sin_yaw, 0.0, cos_yaw]]
    cam_x = cos_yaw * rel_x - sin_yaw * rel_z
    cam_y = rel_y
    cam_z = sin_yaw * rel_x + cos_yaw * rel_z
    inv_depth = 1.0 / cam_z
    centre = 8.0 * IMG_TILES
    screen_x = focal_length * cam_x * inv_depth + centre
    screen_y = focal_length * cam_y * inv_depth + centre_y
    jacob = [[focal_length * inv_depth, 0.0, -focal_length * cam_x * inv_depth * inv_depth], [0.0, focal_length * inv_depth, -focal_length * cam_y * inv_depth * inv_depth]]
    proj = [[jacob[row_at][0] * view[0][col_at] + jacob[row_at][1] * view[1][col_at] + jacob[row_at][2] * view[2][col_at] for col_at in range(3)] for row_at in range(2)]
    quat_norm = jnp.sqrt(rows[6] * rows[6] + rows[7] * rows[7] + rows[8] * rows[8] + rows[9] * rows[9])
    quat_w = rows[6] / quat_norm
    quat_x = rows[7] / quat_norm
    quat_y = rows[8] / quat_norm
    quat_z = rows[9] / quat_norm
    rotation = [[1.0 - 2.0 * (quat_y * quat_y + quat_z * quat_z), 2.0 * (quat_x * quat_y - quat_w * quat_z), 2.0 * (quat_x * quat_z + quat_w * quat_y)], [2.0 * (quat_x * quat_y + quat_w * quat_z), 1.0 - 2.0 * (quat_x * quat_x + quat_z * quat_z), 2.0 * (quat_y * quat_z - quat_w * quat_x)], [2.0 * (quat_x * quat_z - quat_w * quat_y), 2.0 * (quat_y * quat_z + quat_w * quat_x), 1.0 - 2.0 * (quat_x * quat_x + quat_y * quat_y)]]
    scales = [jnp.exp(rows[3]), jnp.exp(rows[4]), jnp.exp(rows[5])]
    spread = [[(proj[row_at][0] * rotation[0][col_at] + proj[row_at][1] * rotation[1][col_at] + proj[row_at][2] * rotation[2][col_at]) * scales[col_at] for col_at in range(3)] for row_at in range(2)]
    cov_a = spread[0][0] * spread[0][0] + spread[0][1] * spread[0][1] + spread[0][2] * spread[0][2] + dilation
    cov_b = spread[0][0] * spread[1][0] + spread[0][1] * spread[1][1] + spread[0][2] * spread[1][2]
    cov_c = spread[1][0] * spread[1][0] + spread[1][1] * spread[1][1] + spread[1][2] * spread[1][2] + dilation
    determ = cov_a * cov_c - cov_b * cov_b
    distance = jnp.sqrt(rel_x * rel_x + rel_y * rel_y + rel_z * rel_z)
    basis = harmonics(rel_x / distance, rel_y / distance, rel_z / distance)
    colours = []
    for channel in range(3):
        acc_col = 0.5 + 0.0 * rel_x
        for order in range(16):
            acc_col = acc_col + basis[order] * rows[11 + 16 * channel + order]
        colours.append(acc_col)
    opacity = jax.nn.sigmoid(rows[10])
    return jnp.stack([screen_x, screen_y, cov_c / determ, -cov_b / determ, cov_a / determ, opacity, colours[0], colours[1], colours[2]])

def pixel_grid(first_tile, count):
    tile_ids = first_tile + jnp.arange(count).astype(jnp.int32)
    local = jnp.arange(TILE_PIX).astype(jnp.int32)
    pix_x = tile_ids[:, None] % IMG_TILES * tile_side + local[None, :] % tile_side
    pix_y = tile_ids[:, None] // IMG_TILES * tile_side + local[None, :] // tile_side
    return (pix_x.astype(jnp.float32) + 0.5, pix_y.astype(jnp.float32) + 0.5)

def tile_image(chosen, length_here, row_x, row_y):
    live_mask = (jnp.arange(MAXL).astype(jnp.int32) < length_here).astype(jnp.float32)
    off_x = row_x[None, :] - chosen[0][:, None]
    off_y = row_y[None, :] - chosen[1][:, None]
    exponent = -0.5 * (chosen[2][:, None] * off_x * off_x + chosen[4][:, None] * off_y * off_y) - chosen[3][:, None] * off_x * off_y
    alpha_val = live_mask[:, None] * chosen[5][:, None] * jnp.exp(exponent)
    log_keep = jnp.log(1.0 - alpha_val)
    before = jnp.cumsum(log_keep, axis=0) - log_keep
    weight = alpha_val * jnp.exp(before)
    return jnp.einsum('ck,kp->cp', chosen[6:9], weight, precision=lax.Precision.HIGHEST)

def reference(gaussians, moment_one, moment_two, cameras, requests, tile_lists, tile_lengths, cotangent):
    holder = (jnp.arange(TILES) // TILES_DEV).astype(jnp.int32)
    pix_x, pix_y = pixel_grid(0, TILES)
    centre_y = 8.0 * TILES / IMG_TILES

    def total_loss(rows):
        summed = jnp.zeros((), jnp.float32)
        for camera_index in range(CAMERAS):
            screen = screen_of(rows, cameras[camera_index], centre_y)
            slot_ids = tile_lists[camera_index]
            owner = slot_ids // CAP
            global_ids = (owner * G_DEV + requests[camera_index][holder[:, None] * SLOTS + slot_ids]).astype(jnp.int32)

            def per_tile(packed):
                ids_here, length_here, cot_here, row_x, row_y = packed
                chosen = jnp.take(screen, ids_here, axis=1)
                return jnp.sum(cot_here * tile_image(chosen, length_here, row_x, row_y))
            terms = lax.map(jax.checkpoint(per_tile), (global_ids, tile_lengths[camera_index], cotangent[camera_index], pix_x, pix_y))
            summed = summed + jnp.sum(terms)
        return summed
    gradient = jax.grad(total_loss)(gaussians)
    first_new = 0.9 * moment_one + 0.1 * gradient
    second_new = 0.999 * moment_two + 0.001 * gradient * gradient
    updated = gaussians - 0.01 * first_new / (jnp.sqrt(second_new) + 1e-08)
    return (gradient, updated, first_new, second_new)
```

```python
import jax
import jax.numpy as jnp
from jax import lax
from jax.experimental import pallas as pl
from jax.experimental.pallas import tpu as pltpu
from jax.sharding import PartitionSpec as P

f32 = jnp.float32
bf16 = jnp.bfloat16
MESH = pl.DeviceIdType.MESH
N_TILE = 128
N_CAM = 4
OWN = 512
SLOTS = 1024
PIX = 256
GROUP = 256
SHIFT = 32

focal_length = 350.0
dilation = 0.3
sh_zero = 0.28209479177387814
sh_one = 0.4886025119029199
sh_two = [
    1.0925484305920792,
    -1.0925484305920792,
    0.31539156525252005,
    -1.0925484305920792,
    0.5462742152960396,
]
sh_three = [
    -0.5900435899266435,
    2.890611442640554,
    -0.4570457994644658,
    0.3731763325901154,
    -0.4570457994644658,
    1.445305721320277,
    -0.5900435899266435,
]


def harmonics(dir_x, dir_y, dir_z):
    xx = dir_x * dir_x
    yy = dir_y * dir_y
    zz = dir_z * dir_z
    return [
        jnp.full_like(dir_x, sh_zero),
        -sh_one * dir_y,
        sh_one * dir_z,
        -sh_one * dir_x,
        sh_two[0] * dir_x * dir_y,
        sh_two[1] * dir_y * dir_z,
        sh_two[2] * (2.0 * zz - xx - yy),
        sh_two[3] * dir_x * dir_z,
        sh_two[4] * (xx - yy),
        sh_three[0] * dir_y * (3.0 * xx - yy),
        sh_three[1] * dir_x * dir_y * dir_z,
        sh_three[2] * dir_y * (4.0 * zz - xx - yy),
        sh_three[3] * dir_z * (2.0 * zz - 3.0 * xx - 3.0 * yy),
        sh_three[4] * dir_x * (4.0 * zz - xx - yy),
        sh_three[5] * dir_z * (xx - yy),
        sh_three[6] * dir_x * (xx - 3.0 * yy),
    ]


def screen_of(rows, camera, cos_yaw, sin_yaw):
    rel_x = rows[0] - camera[0]
    rel_y = rows[1] - camera[1]
    rel_z = rows[2] - camera[2]
    cam_x = cos_yaw * rel_x - sin_yaw * rel_z
    cam_z = sin_yaw * rel_x + cos_yaw * rel_z
    inv_depth = 1.0 / cam_z
    scaled = focal_length * inv_depth
    screen_x = scaled * cam_x + 128.0
    screen_y = scaled * rel_y + 64.0
    slant_x = -scaled * cam_x * inv_depth
    slant_y = -scaled * rel_y * inv_depth
    proj = [
        [scaled * cos_yaw + slant_x * sin_yaw, None, slant_x * cos_yaw - scaled * sin_yaw],
        [slant_y * sin_yaw, scaled, slant_y * cos_yaw],
    ]
    quat_norm = jnp.sqrt(
        rows[6] * rows[6] + rows[7] * rows[7] + rows[8] * rows[8] + rows[9] * rows[9]
    )
    inv_norm = 1.0 / quat_norm
    quat_w = rows[6] * inv_norm
    quat_x = rows[7] * inv_norm
    quat_y = rows[8] * inv_norm
    quat_z = rows[9] * inv_norm
    rotation = [
        [
            1.0 - 2.0 * (quat_y * quat_y + quat_z * quat_z),
            2.0 * (quat_x * quat_y - quat_w * quat_z),
            2.0 * (quat_x * quat_z + quat_w * quat_y),
        ],
        [
            2.0 * (quat_x * quat_y + quat_w * quat_z),
            1.0 - 2.0 * (quat_x * quat_x + quat_z * quat_z),
            2.0 * (quat_y * quat_z - quat_w * quat_x),
        ],
        [
            2.0 * (quat_x * quat_z - quat_w * quat_y),
            2.0 * (quat_y * quat_z + quat_w * quat_x),
            1.0 - 2.0 * (quat_x * quat_x + quat_y * quat_y),
        ],
    ]
    scales = [jnp.exp(rows[3]), jnp.exp(rows[4]), jnp.exp(rows[5])]
    shape_of = [[rotation[i][j] * scales[j] for j in range(3)] for i in range(3)]
    spread = [
        [proj[0][0] * shape_of[0][j] + proj[0][2] * shape_of[2][j] for j in range(3)],
        [
            proj[1][0] * shape_of[0][j] + proj[1][1] * shape_of[1][j] + proj[1][2] * shape_of[2][j]
            for j in range(3)
        ],
    ]
    cov_a = spread[0][0] ** 2 + spread[0][1] ** 2 + spread[0][2] ** 2 + dilation
    cov_b = spread[0][0] * spread[1][0] + spread[0][1] * spread[1][1] + spread[0][2] * spread[1][2]
    cov_c = spread[1][0] ** 2 + spread[1][1] ** 2 + spread[1][2] ** 2 + dilation
    inv_det = 1.0 / (cov_a * cov_c - cov_b * cov_b)
    inv_dist = 1.0 / jnp.sqrt(rel_x * rel_x + rel_y * rel_y + rel_z * rel_z)
    basis = harmonics(rel_x * inv_dist, rel_y * inv_dist, rel_z * inv_dist)
    colours = []
    for channel in range(3):
        acc_col = 0.5 + basis[0] * rows[11 + 16 * channel]
        for order in range(1, 16):
            acc_col = acc_col + basis[order] * rows[11 + 16 * channel + order]
        colours.append(acc_col)
    return [screen_x, screen_y, cov_c * inv_det, -cov_b * inv_det, cov_a * inv_det, *colours]


def parts_of(value, count):
    out = []
    for _ in range(count):
        part = value.astype(bf16).astype(f32)
        out.append(part)
        value = value - part
    return out


def dot(left, right, dims=((1,), (0,))):
    return lax.dot_general(left, right, (dims, ((), ())), preferred_element_type=f32)


def stack_rows(rows, count):
    width = rows[0].shape[1]
    at = lax.broadcasted_iota(jnp.int32, (count, width), 0)
    out = jnp.zeros((count, width), f32)
    for i, row in enumerate(rows):
        out = jnp.where(at == i, row, out)
    return out


def wait_for(ref, sem):
    pltpu.make_async_copy(ref, ref, sem).wait()


def splat_kernel(
    gauss_ref, camera_ref, req_ref, list_ref, length_ref, cot_ref,
    out_ref,
    ask_out, ask_in, row_out, row_in, grad_out, grad_in, cam_out,
    picked, at_owner, expo, gain, alpha, keep_a, keep_b, before, weight_a, weight_b,
    drop_a, drop_b, behind, wgain, turned,
    *sems,
):
    me = lax.axis_index("tile")
    cam = lax.axis_index("cam")
    high = me // 16
    low = lax.rem(me, 16)

    barrier = pltpu.get_barrier_semaphore()

    @pl.loop(1, N_TILE)
    def _(i):
        pl.semaphore_signal(
            barrier, inc=1, device_id=(lax.rem(me + i, N_TILE), cam), device_id_type=MESH
        )

    for i in range(1, N_CAM):
        pl.semaphore_signal(
            barrier, inc=1, device_id=(me, lax.rem(cam + i, N_CAM)), device_id_type=MESH
        )

    def exchange(src, dst, send_sem, recv_sem, source_of):
        @pl.loop(1, N_TILE)
        def _(i):
            peer = lax.rem(me + i, N_TILE)
            pltpu.make_async_remote_copy(
                src.at[source_of(peer)], dst.at[me], send_sem, recv_sem,
                device_id=(peer, cam), device_id_type=MESH,
            ).start()

    for z in range(8):
        ask_out[z] = req_ref[:, 128 * z : 128 * (z + 1)]
    camera = camera_ref[...]
    heading = camera[:, 3:4]
    cos_yaw = jnp.cos(heading)
    sin_yaw = jnp.sin(heading)
    rows = [gauss_ref[i : i + 1, :] for i in range(59)]
    values = screen_of(
        rows, [camera[:, 0:1], camera[:, 1:2], camera[:, 2:3]], cos_yaw, sin_yaw
    )
    opacity = 1.0 / (1.0 + jnp.exp(-rows[10]))
    zero = jnp.zeros_like(opacity)
    table = stack_rows([*values[:5], opacity, zero, zero, *values[5:]], 16)
    table = jnp.concatenate(parts_of(table, 3), axis=0).astype(bf16)
    cam_rows = stack_rows(
        [jnp.broadcast_to(v, (1, OWN)) for v in
         (camera[:, 0:1], camera[:, 1:2], camera[:, 2:3], cos_yaw, sin_yaw)],
        8,
    )

    pl.semaphore_wait(barrier, N_TILE - 1 + N_CAM - 1)
    exchange(ask_out, ask_in, sems[0], sems[1], lambda peer: peer // 16)
    ask_in[me] = ask_out[high]

    list_row = list_ref[0]
    slot_owner = lax.shift_right_logical(list_row, 3)
    slot_part = jnp.bitwise_and(list_row, 7)
    at_owner[...] = jnp.where(
        lax.broadcasted_iota(jnp.int32, (N_TILE, SLOTS), 0) == slot_owner, 1.0, 0.0
    ).astype(bf16)
    live = (
        lax.broadcasted_iota(jnp.int32, (1, SLOTS), 1) < jnp.broadcast_to(length_ref[...], (1, SLOTS))
    )
    pixel = lax.broadcasted_iota(jnp.int32, (1, PIX), 1)
    loc_x = jnp.bitwise_and(pixel, 15).astype(f32) - 7.5
    loc_y = lax.shift_right_logical(pixel, 4).astype(f32) - 7.5
    basis = stack_rows(
        [loc_x * loc_x, loc_y * loc_y, loc_x * loc_y, loc_x, loc_y, jnp.ones_like(loc_x)], 8
    )
    cot = jnp.concatenate([cot_ref[0, 0], jnp.zeros((5, PIX), f32)], axis=0)
    cot_h, cot_m, cot_l = parts_of(cot, 3)
    wide = jnp.concatenate(
        [basis, basis, basis, cot_h, cot_h, cot_h, cot_m, cot_m, cot_l, jnp.zeros((56, PIX), f32)],
        axis=0,
    )
    wide = jnp.transpose(wide).astype(bf16)
    basis_cols = wide[:, 0:24]
    cot_cols = wide[:, 24:72]
    cot_rows = jnp.concatenate([cot_h, cot_m], axis=0).astype(bf16)
    basis_rows = jnp.concatenate([basis, jnp.zeros_like(basis)], axis=0).astype(bf16)
    up = lax.broadcasted_iota(jnp.int32, (GROUP, GROUP), 0)
    down = lax.broadcasted_iota(jnp.int32, (GROUP, GROUP), 1)
    earlier = jnp.where(up < down, 1.0, 0.0).astype(bf16)
    later = jnp.where(up > down, 1.0, 0.0).astype(bf16)
    ones = jnp.ones((GROUP, 128), bf16)

    wait_for(ask_in.at[pl.ds(0, N_TILE - 1)], sems[1])

    asked = jnp.transpose(ask_in[:, 0, :])
    turned[...] = asked
    asked = turned[pl.ds(pl.multiple_of(low * 8, 8), 8), :]
    own_at = lax.broadcasted_iota(jnp.int32, (OWN, 128), 0)
    for s in range(8):
        picked[:, 128 * s : 128 * (s + 1)] = jnp.where(
            own_at == asked[s : s + 1, :], 1.0, 0.0
        ).astype(bf16)
    found = dot(table, picked[...])
    found = found[0:16] + found[16:32] + found[32:48]
    found = jnp.concatenate([found[:, 128 * s : 128 * (s + 1)] for s in range(8)], axis=0)
    row_out[:, 0, :] = jnp.transpose(found)
    exchange(row_out, row_in, sems[2], sems[3], lambda peer: peer)
    row_in[me] = row_out[me]
    wait_for(row_in.at[pl.ds(0, N_TILE - 1)], sems[3])

    got = jnp.transpose(row_in[:, 0, :])
    got = jnp.concatenate(parts_of(got, 3), axis=0).astype(bf16)
    listed = dot(got, at_owner[...])
    listed = listed[0:128] + listed[128:256] + listed[256:384]
    slot = jnp.zeros((16, SLOTS), f32)
    for s in range(8):
        slot = slot + jnp.where(slot_part == s, listed[16 * s : 16 * (s + 1)], 0.0)
    tile_x = (lax.rem(me, 16) * 16 + 8).astype(f32)
    tile_y = (high * 16 + 8).astype(f32)
    off_x = slot[0:1] - tile_x
    off_y = slot[1:2] - tile_y
    con_a, con_b, con_c = slot[2:3], slot[3:4], slot[4:5]
    op_live = jnp.where(live, slot[5:6], 0.0)
    push_x = con_a * off_x + con_b * off_y
    push_y = con_c * off_y + con_b * off_x
    coef = stack_rows(
        [-0.5 * con_a, -0.5 * con_c, -con_b, push_x, push_y,
         -0.5 * (off_x * push_x + off_y * push_y)],
        8,
    )
    coef = jnp.concatenate(parts_of(coef, 3), axis=0).astype(bf16)
    colour = parts_of(slot[8:16], 3)
    colour = jnp.concatenate(
        [colour[0], colour[1], colour[2], colour[0], colour[1], colour[0]], axis=0
    ).astype(bf16)
    expo[...] = dot(basis_cols, coef)
    gain[...] = dot(cot_cols, colour)

    groups = range(SLOTS // GROUP)

    def blocks(group, step):
        cols = slice(GROUP * group, GROUP * (group + 1))

        @pl.loop(0, PIX // SHIFT)
        def _(i):
            step((pl.ds(pl.multiple_of(i * SHIFT, SHIFT), SHIFT), cols))

    def split_to(value, ref_a, ref_b, at):
        part = value.astype(bf16)
        ref_a[at] = part
        ref_b[at] = (value - part.astype(f32)).astype(bf16)

    for g in groups:
        def opaque(at):
            shade = op_live[:, at[1]] * jnp.exp(expo[at])
            alpha[at] = shade
            split_to(jnp.log(1.0 - shade), keep_a, keep_b, at)

        blocks(g, opaque)

    def total_of(ref_a, ref_b, cols):
        total = dot(ref_a[:, cols], ones) + dot(ref_b[:, cols], ones)
        return jnp.concatenate([total, total], axis=1)

    carried = None
    for g in groups:
        cols = slice(GROUP * g, GROUP * (g + 1))
        inside = dot(keep_a[:, cols], earlier) + dot(keep_b[:, cols], earlier)
        before[:, cols] = inside if carried is None else inside + carried
        if g + 1 < len(groups):
            total = total_of(keep_a, keep_b, cols)
            carried = total if carried is None else carried + total

    for g in groups:
        def weigh(at):
            weight = alpha[at] * jnp.exp(before[at])
            split_to(weight, weight_a, weight_b, at)
            weighted = gain[at] * weight
            wgain[at] = weighted
            split_to(weighted, keep_a, keep_b, at)

        blocks(g, weigh)

    carried = None
    for g in reversed(groups):
        cols = slice(GROUP * g, GROUP * (g + 1))
        inside = dot(keep_a[:, cols], later) + dot(keep_b[:, cols], later)
        behind[:, cols] = inside if carried is None else inside + carried
        if g:
            total = total_of(keep_a, keep_b, cols)
            carried = total if carried is None else carried + total

    for g in groups:
        def drop(at):
            shade = alpha[at]
            split_to(wgain[at] - behind[at] * (shade / (1.0 - shade)), drop_a, drop_b, at)

        blocks(g, drop)

    tint = dot(cot_rows, weight_a[...]) + dot(cot_rows, weight_b[...])
    tint = tint[0:8] + tint[8:16]
    moment = dot(basis_rows, drop_a[...]) + dot(basis_rows, drop_b[...])
    m_xx, m_yy, m_xy = moment[0:1], moment[1:2], moment[2:3]
    m_x, m_y, m_one = moment[3:4], moment[4:5], moment[5:6]
    m_du = m_x - off_x * m_one
    m_dv = m_y - off_y * m_one
    slot_grad = stack_rows(
        [
            con_a * m_du + con_b * m_dv,
            con_c * m_dv + con_b * m_du,
            -0.5 * (m_xx - off_x * (m_x + m_du)),
            -(m_xy - off_x * m_y - off_y * m_du),
            -0.5 * (m_yy - off_y * (m_y + m_dv)),
            m_one,
        ],
        8,
    )
    slot_grad = jnp.concatenate([slot_grad, tint], axis=0)

    spread = jnp.concatenate(
        [jnp.where(slot_part == s, slot_grad, 0.0) for s in range(8)], axis=0
    )
    sums = None
    for part in parts_of(spread, 3):
        term = dot(at_owner[...], part.astype(bf16), ((1,), (1,)))
        sums = term if sums is None else sums + term
    grad_out[:, 0, :] = sums
    exchange(grad_out, grad_in, sems[4], sems[5], lambda peer: peer)
    grad_in[me] = grad_out[me]
    wait_for(grad_in.at[pl.ds(0, N_TILE - 1)], sems[5])

    back = jnp.transpose(grad_in[:, 0, :])
    back = jnp.concatenate([back[16 * s : 16 * (s + 1)] for s in range(8)], axis=1)
    back = jnp.concatenate(parts_of(back, 3), axis=0).astype(bf16)
    back = dot(back, picked[...], ((1,), (1,)))
    back = back[0:16] + back[16:32] + back[32:48]
    cam_out[0:16] = back
    cam_out[16:24] = cam_rows

    for i in range(1, N_CAM):
        pltpu.make_async_remote_copy(
            cam_out, out_ref.at[cam], sems[6], sems[7],
            device_id=(me, lax.rem(cam + i, N_CAM)), device_id_type=MESH,
        ).start()
    out_ref[cam] = cam_out[...]
    wait_for(out_ref.at[pl.ds(0, N_CAM - 1)], sems[7])
    wait_for(out_ref.at[pl.ds(0, N_CAM - 1)], sems[6])
    for sem in (sems[0], sems[2], sems[4]):
        wait_for(row_in.at[pl.ds(0, N_TILE - 1)], sem)


def update_kernel(gauss_ref, one_ref, two_ref, back_ref, grad_ref, new_ref, first_ref, second_ref):
    rows = [gauss_ref[i : i + 1, :] for i in range(59)]
    cams = [back_ref[:, 16 + i, :] for i in range(5)]

    def values_of(wanted):
        full = [*wanted[:10], None, *wanted[10:]]
        return screen_of(full, cams[:3], cams[3], cams[4])

    wanted = [*rows[:10], *rows[11:]]
    _, pull = jax.vjp(values_of, wanted)
    order = [0, 1, 2, 3, 4, 8, 9, 10]
    (grads,) = pull([back_ref[:, i, :] for i in order])
    opacity = 1.0 / (1.0 + jnp.exp(-rows[10]))
    shade = jnp.sum(back_ref[:, 5, :], axis=0, keepdims=True) * (1.0 - opacity)
    for i, grad in enumerate([*grads[:10], shade, *grads[10:]]):
        grad_ref[i : i + 1, :] = grad
    grad = grad_ref[...]
    first = 0.9 * one_ref[...] + 0.1 * grad
    second = 0.999 * two_ref[...] + 0.001 * grad * grad
    first_ref[...] = first
    second_ref[...] = second
    new_ref[...] = gauss_ref[...] - 0.01 * first / (jnp.sqrt(second) + 1e-08)


def body(gaussians, moment_one, moment_two, cameras, requests, tile_lists, tile_lengths, cotangent):
    vmem = pl.BlockSpec(memory_space=pltpu.VMEM)
    message = (N_TILE, 1, 128)
    plane = (PIX, SLOTS)
    back = pl.pallas_call(
        splat_kernel,
        out_shape=jax.ShapeDtypeStruct((N_CAM, 24, OWN), f32),
        in_specs=[vmem] * 6,
        out_specs=vmem,
        scratch_shapes=[
            pltpu.VMEM((8, 1, 128), jnp.int32),
            pltpu.VMEM(message, jnp.int32),
            pltpu.VMEM(message, f32),
            pltpu.VMEM(message, f32),
            pltpu.VMEM(message, f32),
            pltpu.VMEM(message, f32),
            pltpu.VMEM((24, OWN), f32),
            pltpu.VMEM((OWN, SLOTS), bf16),
            pltpu.VMEM((N_TILE, SLOTS), bf16),
            pltpu.VMEM(plane, f32),
            pltpu.VMEM(plane, f32),
            pltpu.VMEM(plane, f32),
            pltpu.VMEM(plane, bf16),
            pltpu.VMEM(plane, bf16),
            pltpu.VMEM(plane, f32),
            pltpu.VMEM(plane, bf16),
            pltpu.VMEM(plane, bf16),
            pltpu.VMEM(plane, bf16),
            pltpu.VMEM(plane, bf16),
            pltpu.VMEM(plane, f32),
            pltpu.VMEM(plane, f32),
            pltpu.VMEM((128, 128), jnp.int32),
        ]
        + [pltpu.SemaphoreType.DMA] * 8,
        compiler_params=pltpu.CompilerParams(
            collective_id=0, has_side_effects=True, vmem_limit_bytes=40 * 1024 * 1024
        ),
        name="splat",
    )(gaussians, cameras, requests, tile_lists, tile_lengths, cotangent)
    leaf = jax.ShapeDtypeStruct(gaussians.shape, f32)
    return pl.pallas_call(
        update_kernel,
        out_shape=(leaf, leaf, leaf, leaf),
        in_specs=[vmem] * 4,
        out_specs=(vmem, vmem, vmem, vmem),
        compiler_params=pltpu.CompilerParams(vmem_limit_bytes=32 * 1024 * 1024),
        name="update",
    )(gaussians, moment_one, moment_two, back)


def solution(mesh):
    return jax.shard_map(
        body,
        mesh=mesh,
        in_specs=(
            P(None, "tile"),
            P(None, "tile"),
            P(None, "tile"),
            P("cam", None),
            P("cam", "tile"),
            P("cam", "tile", None),
            P("cam", "tile"),
            P("cam", "tile", None, None),
        ),
        out_specs=(P(None, "tile"), P(None, "tile"), P(None, "tile"), P(None, "tile")),
        check_vma=False,
    )
```

```python
import jax
import jax.numpy as jnp
from jax import lax
from jax.experimental import pallas as pl
from jax.experimental.pallas import tpu as pltpu
from jax.sharding import PartitionSpec as P

f32 = jnp.float32
bf16 = jnp.bfloat16
MESH = pl.DeviceIdType.MESH
N_TILE = 128
N_CAM = 4
OWN = 512
SLOTS = 1024
PIX = 256
GROUP = 256
SHIFT = 32

focal_length = 350.0
dilation = 0.3
sh_zero = 0.28209479177387814
sh_one = 0.4886025119029199
sh_two = [
    1.0925484305920792,
    -1.0925484305920792,
    0.31539156525252005,
    -1.0925484305920792,
    0.5462742152960396,
]
sh_three = [
    -0.5900435899266435,
    2.890611442640554,
    -0.4570457994644658,
    0.3731763325901154,
    -0.4570457994644658,
    1.445305721320277,
    -0.5900435899266435,
]


def harmonics(dir_x, dir_y, dir_z):
    xx = dir_x * dir_x
    yy = dir_y * dir_y
    zz = dir_z * dir_z
    return [
        jnp.full_like(dir_x, sh_zero),
        -sh_one * dir_y,
        sh_one * dir_z,
        -sh_one * dir_x,
        sh_two[0] * dir_x * dir_y,
        sh_two[1] * dir_y * dir_z,
        sh_two[2] * (2.0 * zz - xx - yy),
        sh_two[3] * dir_x * dir_z,
        sh_two[4] * (xx - yy),
        sh_three[0] * dir_y * (3.0 * xx - yy),
        sh_three[1] * dir_x * dir_y * dir_z,
        sh_three[2] * dir_y * (4.0 * zz - xx - yy),
        sh_three[3] * dir_z * (2.0 * zz - 3.0 * xx - 3.0 * yy),
        sh_three[4] * dir_x * (4.0 * zz - xx - yy),
        sh_three[5] * dir_z * (xx - yy),
        sh_three[6] * dir_x * (xx - 3.0 * yy),
    ]


def screen_of(rows, camera, cos_yaw, sin_yaw):
    rel_x = rows[0] - camera[0]
    rel_y = rows[1] - camera[1]
    rel_z = rows[2] - camera[2]
    cam_x = cos_yaw * rel_x - sin_yaw * rel_z
    cam_z = sin_yaw * rel_x + cos_yaw * rel_z
    inv_depth = 1.0 / cam_z
    scaled = focal_length * inv_depth
    screen_x = scaled * cam_x + 128.0
    screen_y = scaled * rel_y + 64.0
    slant_x = -scaled * cam_x * inv_depth
    slant_y = -scaled * rel_y * inv_depth
    proj = [
        [scaled * cos_yaw + slant_x * sin_yaw, None, slant_x * cos_yaw - scaled * sin_yaw],
        [slant_y * sin_yaw, scaled, slant_y * cos_yaw],
    ]
    quat_norm = jnp.sqrt(
        rows[6] * rows[6] + rows[7] * rows[7] + rows[8] * rows[8] + rows[9] * rows[9]
    )
    inv_norm = 1.0 / quat_norm
    quat_w = rows[6] * inv_norm
    quat_x = rows[7] * inv_norm
    quat_y = rows[8] * inv_norm
    quat_z = rows[9] * inv_norm
    rotation = [
        [
            1.0 - 2.0 * (quat_y * quat_y + quat_z * quat_z),
            2.0 * (quat_x * quat_y - quat_w * quat_z),
            2.0 * (quat_x * quat_z + quat_w * quat_y),
        ],
        [
            2.0 * (quat_x * quat_y + quat_w * quat_z),
            1.0 - 2.0 * (quat_x * quat_x + quat_z * quat_z),
            2.0 * (quat_y * quat_z - quat_w * quat_x),
        ],
        [
            2.0 * (quat_x * quat_z - quat_w * quat_y),
            2.0 * (quat_y * quat_z + quat_w * quat_x),
            1.0 - 2.0 * (quat_x * quat_x + quat_y * quat_y),
        ],
    ]
    scales = [jnp.exp(rows[3]), jnp.exp(rows[4]), jnp.exp(rows[5])]
    shape_of = [[rotation[i][j] * scales[j] for j in range(3)] for i in range(3)]
    spread = [
        [proj[0][0] * shape_of[0][j] + proj[0][2] * shape_of[2][j] for j in range(3)],
        [
            proj[1][0] * shape_of[0][j] + proj[1][1] * shape_of[1][j] + proj[1][2] * shape_of[2][j]
            for j in range(3)
        ],
    ]
    cov_a = spread[0][0] ** 2 + spread[0][1] ** 2 + spread[0][2] ** 2 + dilation
    cov_b = spread[0][0] * spread[1][0] + spread[0][1] * spread[1][1] + spread[0][2] * spread[1][2]
    cov_c = spread[1][0] ** 2 + spread[1][1] ** 2 + spread[1][2] ** 2 + dilation
    inv_det = 1.0 / (cov_a * cov_c - cov_b * cov_b)
    inv_dist = 1.0 / jnp.sqrt(rel_x * rel_x + rel_y * rel_y + rel_z * rel_z)
    basis = harmonics(rel_x * inv_dist, rel_y * inv_dist, rel_z * inv_dist)
    colours = []
    for channel in range(3):
        acc_col = 0.5 + basis[0] * rows[11 + 16 * channel]
        for order in range(1, 16):
            acc_col = acc_col + basis[order] * rows[11 + 16 * channel + order]
        colours.append(acc_col)
    return [screen_x, screen_y, cov_c * inv_det, -cov_b * inv_det, cov_a * inv_det, *colours]


def parts_of(value, count):
    out = []
    for _ in range(count):
        part = value.astype(bf16).astype(f32)
        out.append(part)
        value = value - part
    return out


def dot(left, right, dims=((1,), (0,))):
    return lax.dot_general(left, right, (dims, ((), ())), preferred_element_type=f32)


def stack_rows(rows, count):
    width = rows[0].shape[1]
    at = lax.broadcasted_iota(jnp.int32, (count, width), 0)
    out = jnp.zeros((count, width), f32)
    for i, row in enumerate(rows):
        out = jnp.where(at == i, row, out)
    return out


def wait_for(ref, sem):
    pltpu.make_async_copy(ref, ref, sem).wait()


def splat_kernel(
    gauss_any, camera_any, req_any, list_any, length_any, cot_any,
    out_ref,
    gauss_ref, camera_ref, req_ref, list_ref, length_ref, cot_ref,
    ask_out, ask_in, row_out, row_in, grad_out, grad_in, cam_out,
    picked, at_owner, expo, gain, alpha, keep_a, keep_b, before, weight_a, weight_b,
    drop_a, drop_b, behind, wgain, turned,
    *sems,
):
    me = lax.axis_index("tile")
    cam = lax.axis_index("cam")
    high = me // 16
    low = lax.rem(me, 16)

    def peers(action):
        for step in (4, 3, 5, 2, 6, 1, 7, 0):
            row = jnp.bitwise_and(high + step, 7)
            for start, end in ((8, 16), (0, 8)) if step else ((8, 16), (1, 8)):

                @pl.loop(start, end)
                def _(i):
                    action(row * 16 + jnp.bitwise_and(low + i, 15), row)

    barrier = pltpu.get_barrier_semaphore()
    peers(
        lambda peer, row: pl.semaphore_signal(
            barrier, inc=1, device_id=(peer, cam), device_id_type=MESH
        )
    )
    for i in range(1, N_CAM):
        pl.semaphore_signal(
            barrier, inc=1, device_id=(me, lax.rem(cam + i, N_CAM)), device_id_type=MESH
        )
    loads = [
        pltpu.make_async_copy(src, dst, sem)
        for src, dst, sem in zip(
            (gauss_any, camera_any, req_any, list_any, length_any, cot_any),
            (gauss_ref, camera_ref, req_ref, list_ref, length_ref, cot_ref),
            sems[8:14],
            strict=True,
        )
    ]
    for load in loads:
        load.start()

    def exchange(src, dst, send_sem, recv_sem, by_row=False):
        def send(peer, row):
            pltpu.make_async_remote_copy(
                src.at[row if by_row else peer], dst.at[me], send_sem, recv_sem,
                device_id=(peer, cam), device_id_type=MESH,
            ).start()

        peers(send)

    for load in loads:
        load.wait()
    for z in range(8):
        ask_out[z] = req_ref[:, 128 * z : 128 * (z + 1)]
    camera = camera_ref[...]
    heading = camera[:, 3:4]
    cos_yaw = jnp.cos(heading)
    sin_yaw = jnp.sin(heading)
    rows = [gauss_ref[i : i + 1, :] for i in range(59)]
    values = screen_of(
        rows, [camera[:, 0:1], camera[:, 1:2], camera[:, 2:3]], cos_yaw, sin_yaw
    )
    opacity = 1.0 / (1.0 + jnp.exp(-rows[10]))
    zero = jnp.zeros_like(opacity)
    table = stack_rows([*values[:5], opacity, zero, zero, *values[5:]], 16)
    table = jnp.concatenate(parts_of(table, 3), axis=0).astype(bf16)
    cam_rows = stack_rows(
        [jnp.broadcast_to(v, (1, OWN)) for v in
         (camera[:, 0:1], camera[:, 1:2], camera[:, 2:3], cos_yaw, sin_yaw)],
        8,
    )

    pl.semaphore_wait(barrier, N_TILE - 1 + N_CAM - 1)
    exchange(ask_out, ask_in, sems[0], sems[1], by_row=True)
    ask_in[me] = ask_out[high]

    list_row = list_ref[...]
    slot_owner = lax.shift_right_logical(list_row, 3)
    slot_part = jnp.bitwise_and(list_row, 7)
    at_owner[...] = jnp.where(
        lax.broadcasted_iota(jnp.int32, (N_TILE, SLOTS), 0) == slot_owner, 1.0, 0.0
    ).astype(bf16)
    live = (
        lax.broadcasted_iota(jnp.int32, (1, SLOTS), 1) < jnp.broadcast_to(length_ref[...], (1, SLOTS))
    )
    pixel = lax.broadcasted_iota(jnp.int32, (1, PIX), 1)
    loc_x = jnp.bitwise_and(pixel, 15).astype(f32) - 7.5
    loc_y = lax.shift_right_logical(pixel, 4).astype(f32) - 7.5
    basis = stack_rows(
        [loc_x * loc_x, loc_y * loc_y, loc_x * loc_y, loc_x, loc_y, jnp.ones_like(loc_x)], 8
    )
    cot = stack_rows([cot_ref[0], cot_ref[1], cot_ref[2]], 8)
    cot_h, cot_m, cot_l = parts_of(cot, 3)
    wide = jnp.concatenate(
        [basis, basis, basis, cot_h, cot_h, cot_h, cot_m, cot_m, cot_l, jnp.zeros((56, PIX), f32)],
        axis=0,
    )
    wide = jnp.transpose(wide).astype(bf16)
    basis_cols = wide[:, 0:24]
    cot_cols = wide[:, 24:72]
    cot_rows = jnp.concatenate([cot_h, cot_m], axis=0).astype(bf16)
    basis_rows = jnp.concatenate([basis, jnp.zeros_like(basis)], axis=0).astype(bf16)
    up = lax.broadcasted_iota(jnp.int32, (GROUP, GROUP), 0)
    down = lax.broadcasted_iota(jnp.int32, (GROUP, GROUP), 1)
    earlier = jnp.where(up < down, 1.0, 0.0).astype(bf16)
    later = jnp.where(up > down, 1.0, 0.0).astype(bf16)
    ones = jnp.ones((GROUP, 128), bf16)

    wait_for(ask_in.at[pl.ds(0, N_TILE - 1)], sems[1])

    asked = jnp.transpose(ask_in[:, 0, :])
    turned[...] = asked
    asked = turned[pl.ds(pl.multiple_of(low * 8, 8), 8), :]
    own_at = lax.broadcasted_iota(jnp.int32, (OWN, 128), 0)
    for s in range(8):
        picked[:, 128 * s : 128 * (s + 1)] = jnp.where(
            own_at == asked[s : s + 1, :], 1.0, 0.0
        ).astype(bf16)
    found = dot(table, picked[...])
    found = found[0:16] + found[16:32] + found[32:48]
    found = jnp.concatenate([found[:, 128 * s : 128 * (s + 1)] for s in range(8)], axis=0)
    row_out[:, 0, :] = jnp.transpose(found)
    exchange(row_out, row_in, sems[2], sems[3])
    row_in[me] = row_out[me]
    wait_for(row_in.at[pl.ds(0, N_TILE - 1)], sems[3])

    got = jnp.transpose(row_in[:, 0, :])
    got = jnp.concatenate(parts_of(got, 3), axis=0).astype(bf16)
    listed = dot(got, at_owner[...])
    listed = listed[0:128] + listed[128:256] + listed[256:384]
    slot = jnp.zeros((16, SLOTS), f32)
    for s in range(8):
        slot = slot + jnp.where(slot_part == s, listed[16 * s : 16 * (s + 1)], 0.0)
    tile_x = (lax.rem(me, 16) * 16 + 8).astype(f32)
    tile_y = (high * 16 + 8).astype(f32)
    off_x = slot[0:1] - tile_x
    off_y = slot[1:2] - tile_y
    con_a, con_b, con_c = slot[2:3], slot[3:4], slot[4:5]
    op_live = jnp.where(live, slot[5:6], 0.0)
    push_x = con_a * off_x + con_b * off_y
    push_y = con_c * off_y + con_b * off_x
    coef = stack_rows(
        [-0.5 * con_a, -0.5 * con_c, -con_b, push_x, push_y,
         -0.5 * (off_x * push_x + off_y * push_y)],
        8,
    )
    coef = jnp.concatenate(parts_of(coef, 3), axis=0).astype(bf16)
    colour = parts_of(slot[8:16], 3)
    colour = jnp.concatenate(
        [colour[0], colour[1], colour[2], colour[0], colour[1], colour[0]], axis=0
    ).astype(bf16)
    expo[...] = dot(basis_cols, coef)
    gain[...] = dot(cot_cols, colour)

    groups = range(SLOTS // GROUP)

    def blocks(group, step):
        cols = slice(GROUP * group, GROUP * (group + 1))

        @pl.loop(0, PIX // SHIFT)
        def _(i):
            step((pl.ds(pl.multiple_of(i * SHIFT, SHIFT), SHIFT), cols))

    def split_to(value, ref_a, ref_b, at):
        part = value.astype(bf16)
        ref_a[at] = part
        ref_b[at] = (value - part.astype(f32)).astype(bf16)

    for g in groups:
        def opaque(at):
            shade = op_live[:, at[1]] * jnp.exp(expo[at])
            alpha[at] = shade
            split_to(jnp.log(1.0 - shade), keep_a, keep_b, at)

        blocks(g, opaque)

    def total_of(ref_a, ref_b, cols):
        total = dot(ref_a[:, cols], ones) + dot(ref_b[:, cols], ones)
        return jnp.concatenate([total, total], axis=1)

    carried = None
    for g in groups:
        cols = slice(GROUP * g, GROUP * (g + 1))
        inside = dot(keep_a[:, cols], earlier) + dot(keep_b[:, cols], earlier)
        before[:, cols] = inside if carried is None else inside + carried
        if g + 1 < len(groups):
            total = total_of(keep_a, keep_b, cols)
            carried = total if carried is None else carried + total

    for g in groups:
        def weigh(at):
            weight = alpha[at] * jnp.exp(before[at])
            split_to(weight, weight_a, weight_b, at)
            weighted = gain[at] * weight
            wgain[at] = weighted
            split_to(weighted, keep_a, keep_b, at)

        blocks(g, weigh)

    carried = None
    for g in reversed(groups):
        cols = slice(GROUP * g, GROUP * (g + 1))
        inside = dot(keep_a[:, cols], later) + dot(keep_b[:, cols], later)
        behind[:, cols] = inside if carried is None else inside + carried
        if g:
            total = total_of(keep_a, keep_b, cols)
            carried = total if carried is None else carried + total

    for g in groups:
        def drop(at):
            shade = alpha[at]
            split_to(wgain[at] - behind[at] * (shade / (1.0 - shade)), drop_a, drop_b, at)

        blocks(g, drop)

    tint = dot(cot_rows, weight_a[...]) + dot(cot_rows, weight_b[...])
    tint = tint[0:8] + tint[8:16]
    moment = dot(basis_rows, drop_a[...]) + dot(basis_rows, drop_b[...])
    m_xx, m_yy, m_xy = moment[0:1], moment[1:2], moment[2:3]
    m_x, m_y, m_one = moment[3:4], moment[4:5], moment[5:6]
    m_du = m_x - off_x * m_one
    m_dv = m_y - off_y * m_one
    slot_grad = stack_rows(
        [
            con_a * m_du + con_b * m_dv,
            con_c * m_dv + con_b * m_du,
            -0.5 * (m_xx - off_x * (m_x + m_du)),
            -(m_xy - off_x * m_y - off_y * m_du),
            -0.5 * (m_yy - off_y * (m_y + m_dv)),
            m_one,
        ],
        8,
    )
    slot_grad = jnp.concatenate([slot_grad, tint], axis=0)

    spread = jnp.concatenate(
        [jnp.where(slot_part == s, slot_grad, 0.0) for s in range(8)], axis=0
    )
    sums = None
    for part in parts_of(spread, 2):
        term = dot(at_owner[...], part.astype(bf16), ((1,), (1,)))
        sums = term if sums is None else sums + term
    grad_out[:, 0, :] = sums
    exchange(grad_out, grad_in, sems[4], sems[5])
    grad_in[me] = grad_out[me]
    wait_for(grad_in.at[pl.ds(0, N_TILE - 1)], sems[5])

    back = jnp.transpose(grad_in[:, 0, :])
    back = jnp.concatenate([back[16 * s : 16 * (s + 1)] for s in range(8)], axis=1)
    back = jnp.concatenate(parts_of(back, 2), axis=0).astype(bf16)
    back = dot(back, picked[...], ((1,), (1,)))
    back = back[0:16] + back[16:32]
    cam_out[0:16] = back
    cam_out[16:24] = cam_rows

    for i in range(1, N_CAM):
        pltpu.make_async_remote_copy(
            cam_out, out_ref.at[cam], sems[6], sems[7],
            device_id=(me, lax.rem(cam + i, N_CAM)), device_id_type=MESH,
        ).start()
    out_ref[cam] = cam_out[...]
    wait_for(out_ref.at[pl.ds(0, N_CAM - 1)], sems[7])
    wait_for(out_ref.at[pl.ds(0, N_CAM - 1)], sems[6])
    for sem in (sems[0], sems[2], sems[4]):
        wait_for(row_in.at[pl.ds(0, N_TILE - 1)], sem)


def update_kernel(
    gauss_ref, one_ref, two_any, back_ref, grad_ref, new_ref, first_ref, second_ref, two_ref, sem
):
    load = pltpu.make_async_copy(two_any, two_ref, sem)
    load.start()
    rows = [gauss_ref[i : i + 1, :] for i in range(59)]
    cams = [back_ref[:, 16 + i, :] for i in range(5)]

    def values_of(wanted):
        full = [*wanted[:10], None, *wanted[10:]]
        return screen_of(full, cams[:3], cams[3], cams[4])

    wanted = [*rows[:10], *rows[11:]]
    _, pull = jax.vjp(values_of, wanted)
    order = [0, 1, 2, 3, 4, 8, 9, 10]
    (grads,) = pull([back_ref[:, i, :] for i in order])
    opacity = 1.0 / (1.0 + jnp.exp(-rows[10]))
    shade = jnp.sum(back_ref[:, 5, :], axis=0, keepdims=True) * (1.0 - opacity)
    for i, grad in enumerate([*grads[:10], shade, *grads[10:]]):
        grad_ref[i : i + 1, :] = grad
    load.wait()
    grad = grad_ref[...]
    first = 0.9 * one_ref[...] + 0.1 * grad
    second = 0.999 * two_ref[...] + 0.001 * grad * grad
    first_ref[...] = first
    second_ref[...] = second
    new_ref[...] = gauss_ref[...] - 0.01 * first / (jnp.sqrt(second) + 1e-08)


def pin(value):
    return pltpu.with_memory_space_constraint(value, pltpu.HBM)


def body(gaussians, moment_one, moment_two, cameras, requests, tile_lists, tile_lengths, cotangent):
    vmem = pl.BlockSpec(memory_space=pltpu.VMEM)
    message = (N_TILE, 1, 128)
    plane = (PIX, SLOTS)
    back = pl.pallas_call(
        splat_kernel,
        out_shape=pltpu.VMEM((N_CAM, 24, OWN), f32),
        in_specs=[pl.BlockSpec(memory_space=pltpu.HBM)] * 6,
        out_specs=vmem,
        scratch_shapes=[
            pltpu.VMEM(gaussians.shape, f32),
            pltpu.VMEM((1, 4), f32),
            pltpu.VMEM((1, SLOTS), jnp.int32),
            pltpu.VMEM((1, SLOTS), jnp.int32),
            pltpu.VMEM((1, 1), jnp.int32),
            pltpu.VMEM((3, 1, PIX), f32),
            pltpu.VMEM((8, 1, 128), jnp.int32),
            pltpu.VMEM(message, jnp.int32),
            pltpu.VMEM(message, f32),
            pltpu.VMEM(message, f32),
            pltpu.VMEM(message, f32),
            pltpu.VMEM(message, f32),
            pltpu.VMEM((24, OWN), f32),
            pltpu.VMEM((OWN, SLOTS), bf16),
            pltpu.VMEM((N_TILE, SLOTS), bf16),
            pltpu.VMEM(plane, f32),
            pltpu.VMEM(plane, f32),
            pltpu.VMEM(plane, f32),
            pltpu.VMEM(plane, bf16),
            pltpu.VMEM(plane, bf16),
            pltpu.VMEM(plane, f32),
            pltpu.VMEM(plane, bf16),
            pltpu.VMEM(plane, bf16),
            pltpu.VMEM(plane, bf16),
            pltpu.VMEM(plane, bf16),
            pltpu.VMEM(plane, f32),
            pltpu.VMEM(plane, f32),
            pltpu.VMEM((128, 128), jnp.int32),
        ]
        + [pltpu.SemaphoreType.DMA] * 14,
        compiler_params=pltpu.CompilerParams(
            collective_id=0, has_side_effects=True, vmem_limit_bytes=40 * 1024 * 1024
        ),
        name="splat",
    )(
        pin(gaussians), pin(cameras), pin(requests), pin(tile_lists.reshape(1, SLOTS)),
        tile_lengths, pin(cotangent.reshape(3, 1, PIX)),
    )
    leaf = jax.ShapeDtypeStruct(gaussians.shape, f32)
    return pl.pallas_call(
        update_kernel,
        out_shape=(leaf, leaf, leaf, leaf),
        in_specs=[vmem, vmem, pl.BlockSpec(memory_space=pltpu.HBM), vmem],
        out_specs=(vmem, vmem, vmem, vmem),
        scratch_shapes=[pltpu.VMEM(gaussians.shape, f32), pltpu.SemaphoreType.DMA],
        compiler_params=pltpu.CompilerParams(vmem_limit_bytes=32 * 1024 * 1024),
        name="update",
    )(gaussians, moment_one, pin(moment_two), back)


def solution(mesh):
    return jax.shard_map(
        body,
        mesh=mesh,
        in_specs=(
            P(None, "tile"),
            P(None, "tile"),
            P(None, "tile"),
            P("cam", None),
            P("cam", "tile"),
            P("cam", "tile", None),
            P("cam", "tile"),
            P("cam", "tile", None, None),
        ),
        out_specs=(P(None, "tile"), P(None, "tile"), P(None, "tile"), P(None, "tile")),
        check_vma=False,
    )
```

```python
import jax
import jax.numpy as jnp
from jax import lax
from jax.experimental import pallas as pl
from jax.experimental.pallas import tpu as pltpu
from jax.sharding import PartitionSpec as P

f32 = jnp.float32
bf16 = jnp.bfloat16
MESH = pl.DeviceIdType.MESH
N_TILE = 128
N_CAM = 4
OWN = 512
SLOTS = 1024
PIX = 256
GROUP = 256

focal_length = 350.0
dilation = 0.3
sh_zero = 0.28209479177387814
sh_one = 0.4886025119029199
sh_two = [
    1.0925484305920792,
    -1.0925484305920792,
    0.31539156525252005,
    -1.0925484305920792,
    0.5462742152960396,
]
sh_three = [
    -0.5900435899266435,
    2.890611442640554,
    -0.4570457994644658,
    0.3731763325901154,
    -0.4570457994644658,
    1.445305721320277,
    -0.5900435899266435,
]


def harmonics(dir_x, dir_y, dir_z):
    xx = dir_x * dir_x
    yy = dir_y * dir_y
    zz = dir_z * dir_z
    return [
        jnp.full_like(dir_x, sh_zero),
        -sh_one * dir_y,
        sh_one * dir_z,
        -sh_one * dir_x,
        sh_two[0] * dir_x * dir_y,
        sh_two[1] * dir_y * dir_z,
        sh_two[2] * (2.0 * zz - xx - yy),
        sh_two[3] * dir_x * dir_z,
        sh_two[4] * (xx - yy),
        sh_three[0] * dir_y * (3.0 * xx - yy),
        sh_three[1] * dir_x * dir_y * dir_z,
        sh_three[2] * dir_y * (4.0 * zz - xx - yy),
        sh_three[3] * dir_z * (2.0 * zz - 3.0 * xx - 3.0 * yy),
        sh_three[4] * dir_x * (4.0 * zz - xx - yy),
        sh_three[5] * dir_z * (xx - yy),
        sh_three[6] * dir_x * (xx - 3.0 * yy),
    ]


def screen_of(rows, camera, cos_yaw, sin_yaw):
    rel_x = rows[0] - camera[0]
    rel_y = rows[1] - camera[1]
    rel_z = rows[2] - camera[2]
    cam_x = cos_yaw * rel_x - sin_yaw * rel_z
    cam_z = sin_yaw * rel_x + cos_yaw * rel_z
    inv_depth = 1.0 / cam_z
    scaled = focal_length * inv_depth
    screen_x = scaled * cam_x + 128.0
    screen_y = scaled * rel_y + 64.0
    slant_x = -scaled * cam_x * inv_depth
    slant_y = -scaled * rel_y * inv_depth
    proj = [
        [scaled * cos_yaw + slant_x * sin_yaw, None, slant_x * cos_yaw - scaled * sin_yaw],
        [slant_y * sin_yaw, scaled, slant_y * cos_yaw],
    ]
    quat_norm = jnp.sqrt(
        rows[6] * rows[6] + rows[7] * rows[7] + rows[8] * rows[8] + rows[9] * rows[9]
    )
    inv_norm = 1.0 / quat_norm
    quat_w = rows[6] * inv_norm
    quat_x = rows[7] * inv_norm
    quat_y = rows[8] * inv_norm
    quat_z = rows[9] * inv_norm
    rotation = [
        [
            1.0 - 2.0 * (quat_y * quat_y + quat_z * quat_z),
            2.0 * (quat_x * quat_y - quat_w * quat_z),
            2.0 * (quat_x * quat_z + quat_w * quat_y),
        ],
        [
            2.0 * (quat_x * quat_y + quat_w * quat_z),
            1.0 - 2.0 * (quat_x * quat_x + quat_z * quat_z),
            2.0 * (quat_y * quat_z - quat_w * quat_x),
        ],
        [
            2.0 * (quat_x * quat_z - quat_w * quat_y),
            2.0 * (quat_y * quat_z + quat_w * quat_x),
            1.0 - 2.0 * (quat_x * quat_x + quat_y * quat_y),
        ],
    ]
    scales = [jnp.exp(rows[3]), jnp.exp(rows[4]), jnp.exp(rows[5])]
    shape_of = [[rotation[i][j] * scales[j] for j in range(3)] for i in range(3)]
    spread = [
        [proj[0][0] * shape_of[0][j] + proj[0][2] * shape_of[2][j] for j in range(3)],
        [
            proj[1][0] * shape_of[0][j] + proj[1][1] * shape_of[1][j] + proj[1][2] * shape_of[2][j]
            for j in range(3)
        ],
    ]
    cov_a = spread[0][0] ** 2 + spread[0][1] ** 2 + spread[0][2] ** 2 + dilation
    cov_b = spread[0][0] * spread[1][0] + spread[0][1] * spread[1][1] + spread[0][2] * spread[1][2]
    cov_c = spread[1][0] ** 2 + spread[1][1] ** 2 + spread[1][2] ** 2 + dilation
    inv_det = 1.0 / (cov_a * cov_c - cov_b * cov_b)
    inv_dist = 1.0 / jnp.sqrt(rel_x * rel_x + rel_y * rel_y + rel_z * rel_z)
    basis = harmonics(rel_x * inv_dist, rel_y * inv_dist, rel_z * inv_dist)
    colours = []
    for channel in range(3):
        acc_col = 0.5 + basis[0] * rows[11 + 16 * channel]
        for order in range(1, 16):
            acc_col = acc_col + basis[order] * rows[11 + 16 * channel + order]
        colours.append(acc_col)
    return [screen_x, screen_y, cov_c * inv_det, -cov_b * inv_det, cov_a * inv_det, *colours]


def parts_of(value, count):
    out = []
    for _ in range(count):
        part = value.astype(bf16).astype(f32)
        out.append(part)
        value = value - part
    return out


def dot(left, right, dims=((1,), (0,))):
    return lax.dot_general(left, right, (dims, ((), ())), preferred_element_type=f32)


def stack_rows(rows, count):
    width = rows[0].shape[1]
    at = lax.broadcasted_iota(jnp.int32, (count, width), 0)
    out = jnp.zeros((count, width), f32)
    for i, row in enumerate(rows):
        out = jnp.where(at == i, row, out)
    return out


def wait_for(ref, sem):
    pltpu.make_async_copy(ref, ref, sem).wait()


def splat_kernel(
    gauss_any, camera_any, req_any, list_any, length_any, cot_any,
    out_ref,
    gauss_ref, camera_ref, req_ref, list_ref, length_ref, cot_ref,
    ask_out, ask_in, row_out, row_in, grad_out, grad_in, cam_out,
    picked, at_owner, expo, gain, alpha, keep_a, keep_b, before, weight_a, weight_b,
    drop_a, drop_b, behind, wgain, turned, at_owner_t, picked_t,
    *sems,
):
    me = lax.axis_index("tile")
    cam = lax.axis_index("cam")
    high = me // 16
    low = lax.rem(me, 16)

    def peers(action):
        for step in (4, 3, 5, 2, 6, 1, 7, 0):
            row = jnp.bitwise_and(high + step, 7)
            for start, end in ((8, 16), (0, 8)) if step else ((8, 16), (1, 8)):

                @pl.loop(start, end)
                def _(i):
                    action(row * 16 + jnp.bitwise_and(low + i, 15), row)

    barrier = pltpu.get_barrier_semaphore()
    peers(
        lambda peer, row: pl.semaphore_signal(
            barrier, inc=1, device_id=(peer, cam), device_id_type=MESH
        )
    )
    for i in range(1, N_CAM):
        pl.semaphore_signal(
            barrier, inc=1, device_id=(me, lax.rem(cam + i, N_CAM)), device_id_type=MESH
        )
    loads = [
        pltpu.make_async_copy(src, dst, sem)
        for src, dst, sem in zip(
            (gauss_any, camera_any, req_any, list_any, length_any, cot_any),
            (gauss_ref, camera_ref, req_ref, list_ref, length_ref, cot_ref),
            sems[8:14],
            strict=True,
        )
    ]
    for load in loads:
        load.start()

    def exchange(src, dst, send_sem, recv_sem, by_row=False):
        def send(peer, row):
            pltpu.make_async_remote_copy(
                src.at[row if by_row else peer], dst.at[me], send_sem, recv_sem,
                device_id=(peer, cam), device_id_type=MESH,
            ).start()

        peers(send)

    for load in loads:
        load.wait()
    for z in range(8):
        ask_out[z] = req_ref[:, 128 * z : 128 * (z + 1)]
    camera = camera_ref[...]
    heading = camera[:, 3:4]
    cos_yaw = jnp.cos(heading)
    sin_yaw = jnp.sin(heading)
    rows = [gauss_ref[i : i + 1, :] for i in range(59)]
    values = screen_of(
        rows, [camera[:, 0:1], camera[:, 1:2], camera[:, 2:3]], cos_yaw, sin_yaw
    )
    opacity = 1.0 / (1.0 + jnp.exp(-rows[10]))
    zero = jnp.zeros_like(opacity)
    table = stack_rows([*values[:5], opacity, zero, zero, *values[5:]], 16)
    table = jnp.concatenate(
        [part[:, 128 * c : 128 * (c + 1)] for part in parts_of(table, 3) for c in range(OWN // 128)],
        axis=0,
    ).astype(bf16)
    lane = lax.broadcasted_iota(jnp.int32, (1, OWN), 1)
    cam_row = jnp.zeros((1, OWN), f32)
    for i, value in enumerate(
        (camera[:, 0:1], camera[:, 1:2], camera[:, 2:3], cos_yaw, sin_yaw)
    ):
        cam_row = jnp.where(lane == i, value, cam_row)
    cam_out[9] = cam_row

    pl.semaphore_wait(barrier, N_TILE - 1 + N_CAM - 1)
    exchange(ask_out, ask_in, sems[0], sems[1], by_row=True)
    ask_in[me] = ask_out[high]

    list_row = list_ref[...]
    slot_owner = lax.shift_right_logical(list_row, 3)
    slot_part = jnp.bitwise_and(list_row, 7)
    of_owner = jnp.where(
        lax.broadcasted_iota(jnp.int32, (N_TILE, SLOTS), 0) == slot_owner, 1.0, 0.0
    )
    for i in range(3):
        at_owner[N_TILE * i : N_TILE * (i + 1), :] = of_owner.astype(bf16)
    live = (
        lax.broadcasted_iota(jnp.int32, (1, SLOTS), 1) < jnp.broadcast_to(length_ref[...], (1, SLOTS))
    )
    at_owner_t[...] = jnp.transpose(of_owner).astype(bf16)
    pixel = lax.broadcasted_iota(jnp.int32, (1, PIX), 1)
    loc_x = jnp.bitwise_and(pixel, 15).astype(f32) - 7.5
    loc_y = lax.shift_right_logical(pixel, 4).astype(f32) - 7.5
    basis = stack_rows(
        [loc_x * loc_x, loc_y * loc_y, loc_x * loc_y, loc_x, loc_y, jnp.ones_like(loc_x)], 8
    )
    cot = stack_rows([cot_ref[0], cot_ref[1], cot_ref[2]], 8)
    cot_h, cot_m, cot_l = parts_of(cot, 3)
    wide = jnp.concatenate(
        [basis, basis, basis, cot_h, cot_h, cot_h, cot_m, cot_m, cot_l, jnp.zeros((56, PIX), f32)],
        axis=0,
    )
    wide = jnp.transpose(wide).astype(bf16)
    basis_cols = wide[:, 0:24]
    cot_cols = wide[:, 24:72]
    cot_rows = jnp.concatenate([cot_h, cot_m], axis=0).astype(bf16)
    basis_rows = jnp.concatenate([basis, jnp.zeros_like(basis)], axis=0).astype(bf16)
    up = lax.broadcasted_iota(jnp.int32, (GROUP, GROUP), 0)
    down = lax.broadcasted_iota(jnp.int32, (GROUP, GROUP), 1)
    earlier = jnp.where(up < down, 1.0, 0.0).astype(bf16)
    later = jnp.where(up > down, 1.0, 0.0).astype(bf16)
    ones = jnp.ones((GROUP, 128), bf16)

    wait_for(ask_in.at[pl.ds(0, N_TILE - 1)], sems[1])

    asked = jnp.transpose(ask_in[:, 0, :])
    turned[...] = asked
    asked = turned[pl.ds(pl.multiple_of(low * 8, 8), 8), :]
    fine_at = lax.broadcasted_iota(jnp.int32, (128, 128), 0)
    coarse = lax.shift_right_logical(asked, 7)
    coarse = jnp.concatenate([coarse[s : s + 1] for s in range(8)], axis=1)
    asked = jnp.bitwise_and(asked, 127)
    for s in range(8):
        picked[:, 128 * s : 128 * (s + 1)] = jnp.where(
            fine_at == asked[s : s + 1, :], 1.0, 0.0
        ).astype(bf16)
    found = dot(table, picked[...])
    found = found[0:64] + found[64:128] + found[128:192]
    found = sum(
        jnp.where(coarse == c, found[16 * c : 16 * (c + 1)], 0.0) for c in range(OWN // 128)
    )
    found = jnp.concatenate([found[:, 128 * s : 128 * (s + 1)] for s in range(8)], axis=0)
    row_out[:, 0, :] = jnp.transpose(found)
    exchange(row_out, row_in, sems[2], sems[3])
    row_in[me] = row_out[me]
    picked_t[...] = jnp.transpose(picked[...].astype(f32)).astype(bf16)
    wait_for(row_in.at[pl.ds(0, N_TILE - 1)], sems[3])

    got = jnp.transpose(row_in[:, 0, :])
    got = jnp.concatenate(parts_of(got, 3), axis=1).astype(bf16)
    listed = dot(got, at_owner[...])
    slot = jnp.zeros((16, SLOTS), f32)
    for s in range(8):
        slot = slot + jnp.where(slot_part == s, listed[16 * s : 16 * (s + 1)], 0.0)
    tile_x = (lax.rem(me, 16) * 16 + 8).astype(f32)
    tile_y = (high * 16 + 8).astype(f32)
    off_x = slot[0:1] - tile_x
    off_y = slot[1:2] - tile_y
    con_a, con_b, con_c = slot[2:3], slot[3:4], slot[4:5]
    op_live = jnp.where(live, slot[5:6], 0.0)
    push_x = con_a * off_x + con_b * off_y
    push_y = con_c * off_y + con_b * off_x
    coef = stack_rows(
        [-0.5 * con_a, -0.5 * con_c, -con_b, push_x, push_y,
         -0.5 * (off_x * push_x + off_y * push_y)],
        8,
    )
    coef = jnp.concatenate(parts_of(coef, 3), axis=0).astype(bf16)
    colour = parts_of(slot[8:16], 3)
    colour = jnp.concatenate(
        [colour[0], colour[1], colour[2], colour[0], colour[1], colour[0]], axis=0
    ).astype(bf16)
    expo[...] = dot(basis_cols, coef)
    gain[...] = dot(cot_cols, colour)

    groups = range(SLOTS // GROUP)

    def blocks(group, step):
        step((slice(None), slice(GROUP * group, GROUP * (group + 1))))

    def split_to(value, ref_a, ref_b, at):
        part = value.astype(bf16)
        ref_a[at] = part
        ref_b[at] = (value - part.astype(f32)).astype(bf16)

    for g in groups:
        def opaque(at):
            shade = op_live[:, at[1]] * jnp.exp(expo[at])
            alpha[at] = shade
            split_to(jnp.log(1.0 - shade), keep_a, keep_b, at)

        blocks(g, opaque)

    def total_of(ref_a, ref_b, cols):
        total = dot(ref_a[:, cols], ones) + dot(ref_b[:, cols], ones)
        return jnp.concatenate([total, total], axis=1)

    carried = None
    for g in groups:
        cols = slice(GROUP * g, GROUP * (g + 1))
        inside = dot(keep_a[:, cols], earlier) + dot(keep_b[:, cols], earlier)
        before[:, cols] = inside if carried is None else inside + carried
        if g + 1 < len(groups):
            total = total_of(keep_a, keep_b, cols)
            carried = total if carried is None else carried + total

    for g in groups:
        def weigh(at):
            weight = alpha[at] * jnp.exp(before[at])
            split_to(weight, weight_a, weight_b, at)
            weighted = gain[at] * weight
            wgain[at] = weighted
            split_to(weighted, keep_a, keep_b, at)

        blocks(g, weigh)

    carried = None
    for g in reversed(groups):
        cols = slice(GROUP * g, GROUP * (g + 1))
        inside = dot(keep_a[:, cols], later) + dot(keep_b[:, cols], later)
        behind[:, cols] = inside if carried is None else inside + carried
        if g:
            total = total_of(keep_a, keep_b, cols)
            carried = total if carried is None else carried + total

    for g in groups:
        def drop(at):
            shade = alpha[at]
            split_to(wgain[at] - behind[at] * (shade / (1.0 - shade)), drop_a, drop_b, at)

        blocks(g, drop)

    tint = dot(cot_rows, weight_a[...]) + dot(cot_rows, weight_b[...])
    tint = tint[0:8] + tint[8:16]
    moment = dot(basis_rows, drop_a[...]) + dot(basis_rows, drop_b[...])
    m_xx, m_yy, m_xy = moment[0:1], moment[1:2], moment[2:3]
    m_x, m_y, m_one = moment[3:4], moment[4:5], moment[5:6]
    m_du = m_x - off_x * m_one
    m_dv = m_y - off_y * m_one
    slot_grad = stack_rows(
        [
            con_a * m_du + con_b * m_dv,
            con_c * m_dv + con_b * m_du,
            -0.5 * (m_xx - off_x * (m_x + m_du)),
            -(m_xy - off_x * m_y - off_y * m_du),
            -0.5 * (m_yy - off_y * (m_y + m_dv)),
            m_one,
        ],
        8,
    )
    slot_grad = jnp.concatenate([slot_grad, tint], axis=0)

    spread = jnp.concatenate(
        [jnp.where(slot_part == s, slot_grad, 0.0) for s in range(8)], axis=0
    )
    spread = jnp.concatenate(parts_of(spread, 2), axis=0).astype(bf16)
    sums = dot(spread, at_owner_t[...])
    sums = jnp.transpose(sums[0:128] + sums[128:256])
    grad_out[:, 0, :] = sums
    exchange(grad_out, grad_in, sems[4], sems[5])
    grad_in[me] = grad_out[me]
    wait_for(grad_in.at[pl.ds(0, N_TILE - 1)], sems[5])

    back = jnp.transpose(grad_in[:, 0, :])
    back = jnp.concatenate([back[16 * s : 16 * (s + 1)] for s in range(8)], axis=1)
    back = jnp.concatenate(parts_of(back, 2), axis=0)
    back = jnp.concatenate(
        [jnp.where(coarse == c, back, 0.0) for c in range(OWN // 128)], axis=0
    ).astype(bf16)
    back = dot(back, picked_t[...])
    back = jnp.concatenate(
        [back[32 * c : 32 * c + 16] + back[32 * c + 16 : 32 * (c + 1)] for c in range(OWN // 128)],
        axis=1,
    )
    for i, at in enumerate((0, 1, 2, 3, 4, 5, 8, 9, 10)):
        cam_out[i] = back[at : at + 1]

    for i in range(1, N_CAM):
        pltpu.make_async_remote_copy(
            cam_out, out_ref.at[cam], sems[6], sems[7],
            device_id=(me, lax.rem(cam + i, N_CAM)), device_id_type=MESH,
        ).start()
    out_ref[cam] = cam_out[...]
    wait_for(out_ref.at[pl.ds(0, N_CAM - 1)], sems[7])
    wait_for(out_ref.at[pl.ds(0, N_CAM - 1)], sems[6])
    for sem in (sems[0], sems[2], sems[4]):
        wait_for(row_in.at[pl.ds(0, N_TILE - 1)], sem)


def update_kernel(
    gauss_ref, one_any, two_any, back_ref, grad_ref, new_ref, first_ref, second_ref,
    one_ref, two_ref, *sems,
):
    loads = [
        pltpu.make_async_copy(one_any, one_ref, sems[0]),
        pltpu.make_async_copy(two_any, two_ref, sems[1]),
    ]
    for load in loads:
        load.start()
    half = OWN // 2
    first_half = lax.broadcasted_iota(jnp.int32, (8, half), 0) < N_CAM

    def spread(row):
        return jnp.where(first_half, row[:, :half], row[:, half:])

    def gathered(i):
        values = back_ref[:, i, 0, :]
        return jnp.concatenate([values[:, :half], values[:, half:]], axis=0)

    def over_cams(grad):
        return [jnp.sum(grad[at : at + N_CAM], axis=0, keepdims=True) for at in (0, N_CAM)]

    rows = [spread(gauss_ref[i : i + 1, :]) for i in range(59)]
    cam_rows = back_ref[:, 9, 0, 0:128]
    cam_rows = jnp.concatenate([cam_rows, cam_rows], axis=0)
    cams = [cam_rows[:, i : i + 1] for i in range(5)]

    def values_of(wanted):
        full = [*wanted[:10], None, *wanted[10:]]
        return screen_of(full, cams[:3], cams[3], cams[4])

    _, pull = jax.vjp(values_of, [*rows[:10], *rows[11:]])
    (grads,) = pull([gathered(i) for i in (0, 1, 2, 3, 4, 6, 7, 8)])
    shade = gathered(5) * (1.0 - 1.0 / (1.0 + jnp.exp(-rows[10])))
    for i, grad in enumerate([*grads[:10], shade, *grads[10:]]):
        low, high = over_cams(grad)
        grad_ref[i : i + 1, :half] = low
        grad_ref[i : i + 1, half:] = high
    for load in loads:
        load.wait()
    grad = grad_ref[...]
    first = 0.9 * one_ref[...] + 0.1 * grad
    second = 0.999 * two_ref[...] + 0.001 * grad * grad
    first_ref[...] = first
    second_ref[...] = second
    new_ref[...] = gauss_ref[...] - 0.01 * first / (jnp.sqrt(second) + 1e-08)


def pin(value):
    return pltpu.with_memory_space_constraint(value, pltpu.HBM)


def body(gaussians, moment_one, moment_two, cameras, requests, tile_lists, tile_lengths, cotangent):
    vmem = pl.BlockSpec(memory_space=pltpu.VMEM)
    hbm = pl.BlockSpec(memory_space=pltpu.HBM)
    message = (N_TILE, 1, 128)
    plane = (PIX, SLOTS)
    back = pl.pallas_call(
        splat_kernel,
        out_shape=pltpu.VMEM((N_CAM, 10, 1, OWN), f32),
        in_specs=[hbm] * 6,
        out_specs=vmem,
        scratch_shapes=[
            pltpu.VMEM(gaussians.shape, f32),
            pltpu.VMEM((1, 4), f32),
            pltpu.VMEM((1, SLOTS), jnp.int32),
            pltpu.VMEM((1, SLOTS), jnp.int32),
            pltpu.VMEM((1, 1), jnp.int32),
            pltpu.VMEM((3, 1, PIX), f32),
            pltpu.VMEM((8, 1, 128), jnp.int32),
            pltpu.VMEM(message, jnp.int32),
            pltpu.VMEM(message, f32),
            pltpu.VMEM(message, f32),
            pltpu.VMEM(message, f32),
            pltpu.VMEM(message, f32),
            pltpu.VMEM((10, 1, OWN), f32),
            pltpu.VMEM((128, SLOTS), bf16),
            pltpu.VMEM((3 * N_TILE, SLOTS), bf16),
            pltpu.VMEM(plane, f32),
            pltpu.VMEM(plane, f32),
            pltpu.VMEM(plane, f32),
            pltpu.VMEM(plane, bf16),
            pltpu.VMEM(plane, bf16),
            pltpu.VMEM(plane, f32),
            pltpu.VMEM(plane, bf16),
            pltpu.VMEM(plane, bf16),
            pltpu.VMEM(plane, bf16),
            pltpu.VMEM(plane, bf16),
            pltpu.VMEM(plane, f32),
            pltpu.VMEM(plane, f32),
            pltpu.VMEM((128, 128), jnp.int32),
            pltpu.VMEM((SLOTS, N_TILE), bf16),
            pltpu.VMEM((SLOTS, 128), bf16),
        ]
        + [pltpu.SemaphoreType.DMA] * 14,
        compiler_params=pltpu.CompilerParams(
            collective_id=0, has_side_effects=True, vmem_limit_bytes=40 * 1024 * 1024
        ),
        name="splat",
    )(
        pin(gaussians), pin(cameras), pin(requests), pin(tile_lists.reshape(1, SLOTS)),
        tile_lengths, pin(cotangent.reshape(3, 1, PIX)),
    )
    leaf = jax.ShapeDtypeStruct(gaussians.shape, f32)
    return pl.pallas_call(
        update_kernel,
        out_shape=(leaf, leaf, leaf, leaf),
        in_specs=[vmem, hbm, hbm, vmem],
        out_specs=(vmem, vmem, vmem, vmem),
        scratch_shapes=[pltpu.VMEM(gaussians.shape, f32)] * 2 + [pltpu.SemaphoreType.DMA] * 2,
        compiler_params=pltpu.CompilerParams(vmem_limit_bytes=32 * 1024 * 1024),
        name="update",
    )(gaussians, pin(moment_one), pin(moment_two), back)


def solution(mesh):
    return jax.shard_map(
        body,
        mesh=mesh,
        in_specs=(
            P(None, "tile"),
            P(None, "tile"),
            P(None, "tile"),
            P("cam", None),
            P("cam", "tile"),
            P("cam", "tile", None),
            P("cam", "tile"),
            P("cam", "tile", None, None),
        ),
        out_specs=(P(None, "tile"), P(None, "tile"), P(None, "tile"), P(None, "tile")),
        check_vma=False,
    )
```

```python
import jax
import jax.numpy as jnp
from jax import lax
from jax.experimental import pallas as pl
from jax.experimental.pallas import tpu as pltpu
from jax.sharding import PartitionSpec as P

f32 = jnp.float32
bf16 = jnp.bfloat16
MESH = pl.DeviceIdType.MESH
N_TILE = 128
N_CAM = 4
OWN = 512
SLOTS = 1024
PIX = 256
GROUP = 256

focal_length = 350.0
dilation = 0.3
sh_zero = 0.28209479177387814
sh_one = 0.4886025119029199
sh_two = [
    1.0925484305920792,
    -1.0925484305920792,
    0.31539156525252005,
    -1.0925484305920792,
    0.5462742152960396,
]
sh_three = [
    -0.5900435899266435,
    2.890611442640554,
    -0.4570457994644658,
    0.3731763325901154,
    -0.4570457994644658,
    1.445305721320277,
    -0.5900435899266435,
]


def harmonics(dir_x, dir_y, dir_z):
    xx = dir_x * dir_x
    yy = dir_y * dir_y
    zz = dir_z * dir_z
    return [
        jnp.full_like(dir_x, sh_zero),
        -sh_one * dir_y,
        sh_one * dir_z,
        -sh_one * dir_x,
        sh_two[0] * dir_x * dir_y,
        sh_two[1] * dir_y * dir_z,
        sh_two[2] * (2.0 * zz - xx - yy),
        sh_two[3] * dir_x * dir_z,
        sh_two[4] * (xx - yy),
        sh_three[0] * dir_y * (3.0 * xx - yy),
        sh_three[1] * dir_x * dir_y * dir_z,
        sh_three[2] * dir_y * (4.0 * zz - xx - yy),
        sh_three[3] * dir_z * (2.0 * zz - 3.0 * xx - 3.0 * yy),
        sh_three[4] * dir_x * (4.0 * zz - xx - yy),
        sh_three[5] * dir_z * (xx - yy),
        sh_three[6] * dir_x * (xx - 3.0 * yy),
    ]


def screen_of(rows, camera, cos_yaw, sin_yaw):
    rel_x = rows[0] - camera[0]
    rel_y = rows[1] - camera[1]
    rel_z = rows[2] - camera[2]
    cam_x = cos_yaw * rel_x - sin_yaw * rel_z
    cam_z = sin_yaw * rel_x + cos_yaw * rel_z
    inv_depth = 1.0 / cam_z
    scaled = focal_length * inv_depth
    screen_x = scaled * cam_x + 128.0
    screen_y = scaled * rel_y + 64.0
    slant_x = -scaled * cam_x * inv_depth
    slant_y = -scaled * rel_y * inv_depth
    proj = [
        [scaled * cos_yaw + slant_x * sin_yaw, None, slant_x * cos_yaw - scaled * sin_yaw],
        [slant_y * sin_yaw, scaled, slant_y * cos_yaw],
    ]
    quat_norm = jnp.sqrt(
        rows[6] * rows[6] + rows[7] * rows[7] + rows[8] * rows[8] + rows[9] * rows[9]
    )
    inv_norm = 1.0 / quat_norm
    quat_w = rows[6] * inv_norm
    quat_x = rows[7] * inv_norm
    quat_y = rows[8] * inv_norm
    quat_z = rows[9] * inv_norm
    rotation = [
        [
            1.0 - 2.0 * (quat_y * quat_y + quat_z * quat_z),
            2.0 * (quat_x * quat_y - quat_w * quat_z),
            2.0 * (quat_x * quat_z + quat_w * quat_y),
        ],
        [
            2.0 * (quat_x * quat_y + quat_w * quat_z),
            1.0 - 2.0 * (quat_x * quat_x + quat_z * quat_z),
            2.0 * (quat_y * quat_z - quat_w * quat_x),
        ],
        [
            2.0 * (quat_x * quat_z - quat_w * quat_y),
            2.0 * (quat_y * quat_z + quat_w * quat_x),
            1.0 - 2.0 * (quat_x * quat_x + quat_y * quat_y),
        ],
    ]
    scales = [jnp.exp(rows[3]), jnp.exp(rows[4]), jnp.exp(rows[5])]
    shape_of = [[rotation[i][j] * scales[j] for j in range(3)] for i in range(3)]
    spread = [
        [proj[0][0] * shape_of[0][j] + proj[0][2] * shape_of[2][j] for j in range(3)],
        [
            proj[1][0] * shape_of[0][j] + proj[1][1] * shape_of[1][j] + proj[1][2] * shape_of[2][j]
            for j in range(3)
        ],
    ]
    cov_a = spread[0][0] ** 2 + spread[0][1] ** 2 + spread[0][2] ** 2 + dilation
    cov_b = spread[0][0] * spread[1][0] + spread[0][1] * spread[1][1] + spread[0][2] * spread[1][2]
    cov_c = spread[1][0] ** 2 + spread[1][1] ** 2 + spread[1][2] ** 2 + dilation
    inv_det = 1.0 / (cov_a * cov_c - cov_b * cov_b)
    inv_dist = 1.0 / jnp.sqrt(rel_x * rel_x + rel_y * rel_y + rel_z * rel_z)
    basis = harmonics(rel_x * inv_dist, rel_y * inv_dist, rel_z * inv_dist)
    colours = []
    for channel in range(3):
        acc_col = 0.5 + basis[0] * rows[11 + 16 * channel]
        for order in range(1, 16):
            acc_col = acc_col + basis[order] * rows[11 + 16 * channel + order]
        colours.append(acc_col)
    return [screen_x, screen_y, cov_c * inv_det, -cov_b * inv_det, cov_a * inv_det, *colours]


def parts_of(value, count):
    out = []
    for _ in range(count):
        part = value.astype(bf16).astype(f32)
        out.append(part)
        value = value - part
    return out


def dot(left, right, dims=((1,), (0,))):
    return lax.dot_general(left, right, (dims, ((), ())), preferred_element_type=f32)


def stack_rows(rows, count):
    width = rows[0].shape[1]
    at = lax.broadcasted_iota(jnp.int32, (count, width), 0)
    out = jnp.zeros((count, width), f32)
    for i, row in enumerate(rows):
        out = jnp.where(at == i, row, out)
    return out


def wait_for(ref, sem):
    pltpu.make_async_copy(ref, ref, sem).wait()


def splat_kernel(
    gauss_any, camera_any, req_any, list_any, length_any, cot_any, one_any, two_any,
    out_ref, gauss_ref, one_ref, two_ref,
    camera_ref, req_ref, list_ref, cot_ref,
    ask_out, ask_in, row_out, row_in, grad_out, grad_in, cam_out,
    picked, at_owner, expo, gain, alpha, keep_a, keep_b, before, weight_a, weight_b,
    drop_a, drop_b, behind, wgain, turned, at_owner_t, picked_t,
    *sems,
):
    me = lax.axis_index("tile")
    cam = lax.axis_index("cam")
    high = me // 16
    low = lax.rem(me, 16)

    def peers(action):
        for step in (4, 3, 5, 2, 6, 1, 7, 0):
            row = jnp.bitwise_and(high + step, 7)
            for start, end in ((8, 16), (0, 8)) if step else ((8, 16), (1, 8)):

                @pl.loop(start, end)
                def _(i):
                    action(row * 16 + jnp.bitwise_and(low + i, 15), row)

    barrier = pltpu.get_barrier_semaphore()
    peers(
        lambda peer, row: pl.semaphore_signal(
            barrier, inc=1, device_id=(peer, cam), device_id_type=MESH
        )
    )
    for i in range(1, N_CAM):
        pl.semaphore_signal(
            barrier, inc=1, device_id=(me, lax.rem(cam + i, N_CAM)), device_id_type=MESH
        )
    loads = [
        pltpu.make_async_copy(src, dst, sem)
        for src, dst, sem in zip(
            (gauss_any, camera_any, req_any, list_any, cot_any, one_any, two_any),
            (gauss_ref, camera_ref, req_ref, list_ref, cot_ref, one_ref, two_ref),
            sems[8:15],
            strict=True,
        )
    ]
    for load in loads:
        load.start()

    def exchange(src, dst, send_sem, recv_sem, by_row=False):
        def send(peer, row):
            pltpu.make_async_remote_copy(
                src.at[row if by_row else peer], dst.at[me], send_sem, recv_sem,
                device_id=(peer, cam), device_id_type=MESH,
            ).start()

        peers(send)

    for load in loads[:5]:
        load.wait()
    for z in range(8):
        ask_out[z] = req_ref[:, 128 * z : 128 * (z + 1)]
    camera = camera_ref[...]
    heading = camera[:, 3:4]
    cos_yaw = jnp.cos(heading)
    sin_yaw = jnp.sin(heading)
    rows = [gauss_ref[i : i + 1, :] for i in range(59)]
    values = screen_of(
        rows, [camera[:, 0:1], camera[:, 1:2], camera[:, 2:3]], cos_yaw, sin_yaw
    )
    opacity = 1.0 / (1.0 + jnp.exp(-rows[10]))
    zero = jnp.zeros_like(opacity)
    table = stack_rows([*values[:5], opacity, zero, zero, *values[5:]], 16)
    table = jnp.concatenate(
        [part[:, 128 * c : 128 * (c + 1)] for part in parts_of(table, 3) for c in range(OWN // 128)],
        axis=0,
    ).astype(bf16)
    lane = lax.broadcasted_iota(jnp.int32, (1, OWN), 1)
    cam_row = jnp.zeros((1, OWN), f32)
    for i, value in enumerate(
        (camera[:, 0:1], camera[:, 1:2], camera[:, 2:3], cos_yaw, sin_yaw)
    ):
        cam_row = jnp.where(lane == i, value, cam_row)
    cam_out[9] = cam_row

    pl.semaphore_wait(barrier, N_TILE - 1 + N_CAM - 1)
    exchange(ask_out, ask_in, sems[0], sems[1], by_row=True)
    ask_in[me] = ask_out[high]

    list_row = list_ref[...]
    slot_owner = lax.shift_right_logical(list_row, 3)
    slot_part = jnp.bitwise_and(list_row, 7)
    of_owner = jnp.where(
        lax.broadcasted_iota(jnp.int32, (N_TILE, SLOTS), 0) == slot_owner, 1.0, 0.0
    )
    for i in range(3):
        at_owner[N_TILE * i : N_TILE * (i + 1), :] = of_owner.astype(bf16)
    live = (
        lax.broadcasted_iota(jnp.int32, (1, SLOTS), 1) < length_any[0, 0]
    )
    at_owner_t[...] = jnp.transpose(of_owner).astype(bf16)
    pixel = lax.broadcasted_iota(jnp.int32, (1, PIX), 1)
    loc_x = jnp.bitwise_and(pixel, 15).astype(f32) - 7.5
    loc_y = lax.shift_right_logical(pixel, 4).astype(f32) - 7.5
    basis = stack_rows(
        [loc_x * loc_x, loc_y * loc_y, loc_x * loc_y, loc_x, loc_y, jnp.ones_like(loc_x)], 8
    )
    cot = stack_rows([cot_ref[0], cot_ref[1], cot_ref[2]], 8)
    cot_h, cot_m, cot_l = parts_of(cot, 3)
    wide = jnp.concatenate(
        [basis, basis, basis, cot_h, cot_h, cot_h, cot_m, cot_m, cot_l, jnp.zeros((56, PIX), f32)],
        axis=0,
    )
    wide = jnp.transpose(wide).astype(bf16)
    basis_cols = wide[:, 0:24]
    cot_cols = wide[:, 24:72]
    cot_rows = jnp.concatenate([cot_h, cot_m], axis=0).astype(bf16)
    basis_rows = jnp.concatenate([basis, jnp.zeros_like(basis)], axis=0).astype(bf16)
    up = lax.broadcasted_iota(jnp.int32, (GROUP, GROUP), 0)
    down = lax.broadcasted_iota(jnp.int32, (GROUP, GROUP), 1)
    earlier = jnp.where(up < down, 1.0, 0.0).astype(bf16)
    later = jnp.where(up > down, 1.0, 0.0).astype(bf16)

    wait_for(ask_in.at[pl.ds(0, N_TILE - 1)], sems[1])

    asked = jnp.transpose(ask_in[:, 0, :])
    turned[...] = asked
    asked = turned[pl.ds(pl.multiple_of(low * 8, 8), 8), :]
    fine_at = lax.broadcasted_iota(jnp.int32, (128, 128), 0)
    coarse = lax.shift_right_logical(asked, 7)
    coarse = jnp.concatenate([coarse[s : s + 1] for s in range(8)], axis=1)
    asked = jnp.bitwise_and(asked, 127)
    for s in range(8):
        picked[:, 128 * s : 128 * (s + 1)] = jnp.where(
            fine_at == asked[s : s + 1, :], 1.0, 0.0
        ).astype(bf16)
    found = dot(table, picked[...])
    found = found[0:64] + found[64:128] + found[128:192]
    found = sum(
        jnp.where(coarse == c, found[16 * c : 16 * (c + 1)], 0.0) for c in range(OWN // 128)
    )
    found = jnp.concatenate([found[:, 128 * s : 128 * (s + 1)] for s in range(8)], axis=0)
    row_out[:, 0, :] = jnp.transpose(found)
    exchange(row_out, row_in, sems[2], sems[3])
    row_in[me] = row_out[me]
    picked_t[...] = jnp.transpose(picked[...].astype(f32)).astype(bf16)
    wait_for(row_in.at[pl.ds(0, N_TILE - 1)], sems[3])

    got = jnp.transpose(row_in[:, 0, :])
    got = jnp.concatenate(parts_of(got, 3), axis=1).astype(bf16)
    listed = dot(got, at_owner[...])
    slot = jnp.zeros((16, SLOTS), f32)
    for s in range(8):
        slot = slot + jnp.where(slot_part == s, listed[16 * s : 16 * (s + 1)], 0.0)
    tile_x = (lax.rem(me, 16) * 16 + 8).astype(f32)
    tile_y = (high * 16 + 8).astype(f32)
    off_x = slot[0:1] - tile_x
    off_y = slot[1:2] - tile_y
    con_a, con_b, con_c = slot[2:3], slot[3:4], slot[4:5]
    op_live = jnp.where(live, slot[5:6], 0.0)
    push_x = con_a * off_x + con_b * off_y
    push_y = con_c * off_y + con_b * off_x
    coef = stack_rows(
        [-0.5 * con_a, -0.5 * con_c, -con_b, push_x, push_y,
         -0.5 * (off_x * push_x + off_y * push_y)],
        8,
    )
    coef = jnp.concatenate(parts_of(coef, 3), axis=0).astype(bf16)
    colour = parts_of(slot[8:16], 3)
    colour = jnp.concatenate(
        [colour[0], colour[1], colour[2], colour[0], colour[1], colour[0]], axis=0
    ).astype(bf16)
    expo[...] = dot(basis_cols, coef)
    gain[...] = dot(cot_cols, colour)

    groups = range(SLOTS // GROUP)

    def blocks(group, step):
        step((slice(None), slice(GROUP * group, GROUP * (group + 1))))

    def split_to(value, ref_a, ref_b, at):
        part = value.astype(bf16)
        ref_a[at] = part
        ref_b[at] = (value - part.astype(f32)).astype(bf16)

    for g in groups:
        def opaque(at):
            shade = op_live[:, at[1]] * jnp.exp(expo[at])
            alpha[at] = shade
            split_to(jnp.log(1.0 - shade), keep_a, keep_b, at)

        blocks(g, opaque)

    def edge_of(inside, ref_a, ref_b, at):
        own = ref_a[:, at : at + 1].astype(f32) + ref_b[:, at : at + 1].astype(f32)
        edge = at % GROUP
        return jnp.broadcast_to(inside[:, edge : edge + 1] + own, (PIX, GROUP))

    carried = None
    for g in groups:
        cols = slice(GROUP * g, GROUP * (g + 1))
        inside = dot(keep_a[:, cols], earlier) + dot(keep_b[:, cols], earlier)
        if carried is not None:
            inside = inside + carried
        before[:, cols] = inside
        if g + 1 < len(groups):
            carried = edge_of(inside, keep_a, keep_b, GROUP * (g + 1) - 1)

    for g in groups:
        def weigh(at):
            weight = alpha[at] * jnp.exp(before[at])
            split_to(weight, weight_a, weight_b, at)
            weighted = gain[at] * weight
            wgain[at] = weighted
            split_to(weighted, keep_a, keep_b, at)

        blocks(g, weigh)

    carried = None
    for g in reversed(groups):
        cols = slice(GROUP * g, GROUP * (g + 1))
        inside = dot(keep_a[:, cols], later) + dot(keep_b[:, cols], later)
        if carried is not None:
            inside = inside + carried
        behind[:, cols] = inside
        if g:
            carried = edge_of(inside, keep_a, keep_b, GROUP * g)

    for g in groups:
        def drop(at):
            shade = alpha[at]
            split_to(wgain[at] - behind[at] * (shade / (1.0 - shade)), drop_a, drop_b, at)

        blocks(g, drop)

    tint = dot(cot_rows, weight_a[...]) + dot(cot_rows, weight_b[...])
    tint = tint[0:8] + tint[8:16]
    moment = dot(basis_rows, drop_a[...]) + dot(basis_rows, drop_b[...])
    m_xx, m_yy, m_xy = moment[0:1], moment[1:2], moment[2:3]
    m_x, m_y, m_one = moment[3:4], moment[4:5], moment[5:6]
    m_du = m_x - off_x * m_one
    m_dv = m_y - off_y * m_one
    slot_grad = stack_rows(
        [
            con_a * m_du + con_b * m_dv,
            con_c * m_dv + con_b * m_du,
            -0.5 * (m_xx - off_x * (m_x + m_du)),
            -(m_xy - off_x * m_y - off_y * m_du),
            -0.5 * (m_yy - off_y * (m_y + m_dv)),
            m_one,
        ],
        8,
    )
    slot_grad = jnp.concatenate([slot_grad, tint], axis=0)

    spread = jnp.concatenate(
        [jnp.where(slot_part == s, slot_grad, 0.0) for s in range(8)], axis=0
    )
    spread = jnp.concatenate(parts_of(spread, 2), axis=0).astype(bf16)
    sums = dot(spread, at_owner_t[...])
    sums = jnp.transpose(sums[0:128] + sums[128:256])
    grad_out[:, 0, :] = sums
    exchange(grad_out, grad_in, sems[4], sems[5])
    grad_in[me] = grad_out[me]
    wait_for(grad_in.at[pl.ds(0, N_TILE - 1)], sems[5])

    back = jnp.transpose(grad_in[:, 0, :])
    back = jnp.concatenate([back[16 * s : 16 * (s + 1)] for s in range(8)], axis=1)
    back = jnp.concatenate(parts_of(back, 2), axis=0)
    back = jnp.concatenate(
        [jnp.where(coarse == c, back, 0.0) for c in range(OWN // 128)], axis=0
    ).astype(bf16)
    back = dot(back, picked_t[...])
    back = jnp.concatenate(
        [back[32 * c : 32 * c + 16] + back[32 * c + 16 : 32 * (c + 1)] for c in range(OWN // 128)],
        axis=1,
    )
    for i, at in enumerate((0, 1, 2, 3, 4, 5, 8, 9, 10)):
        cam_out[i] = back[at : at + 1]

    for i in range(1, N_CAM):
        pltpu.make_async_remote_copy(
            cam_out, out_ref.at[cam], sems[6], sems[7],
            device_id=(me, lax.rem(cam + i, N_CAM)), device_id_type=MESH,
        ).start()
    out_ref[cam] = cam_out[...]
    wait_for(out_ref.at[pl.ds(0, N_CAM - 1)], sems[7])
    wait_for(out_ref.at[pl.ds(0, N_CAM - 1)], sems[6])
    for load in loads[5:]:
        load.wait()
    for sem in (sems[0], sems[2], sems[4]):
        wait_for(row_in.at[pl.ds(0, N_TILE - 1)], sem)


def update_kernel(gauss_ref, one_ref, two_ref, back_ref, grad_ref, new_ref, first_ref, second_ref):
    half = OWN // 2
    first_half = lax.broadcasted_iota(jnp.int32, (8, half), 0) < N_CAM

    def spread(row):
        return jnp.where(first_half, row[:, :half], row[:, half:])

    def gathered(i):
        values = back_ref[:, i, 0, :]
        return jnp.concatenate([values[:, :half], values[:, half:]], axis=0)

    def over_cams(grad):
        return [jnp.sum(grad[at : at + N_CAM], axis=0, keepdims=True) for at in (0, N_CAM)]

    rows = [spread(gauss_ref[i : i + 1, :]) for i in range(59)]
    cam_rows = back_ref[:, 9, 0, 0:128]
    cam_rows = jnp.concatenate([cam_rows, cam_rows], axis=0)
    cams = [cam_rows[:, i : i + 1] for i in range(5)]

    def values_of(wanted):
        full = [*wanted[:10], None, *wanted[10:]]
        return screen_of(full, cams[:3], cams[3], cams[4])

    _, pull = jax.vjp(values_of, [*rows[:10], *rows[11:]])
    (grads,) = pull([gathered(i) for i in (0, 1, 2, 3, 4, 6, 7, 8)])
    shade = gathered(5) * (1.0 - 1.0 / (1.0 + jnp.exp(-rows[10])))
    for i, grad in enumerate([*grads[:10], shade, *grads[10:]]):
        low, high = over_cams(grad)
        grad_ref[i : i + 1, :half] = low
        grad_ref[i : i + 1, half:] = high
    grad = grad_ref[...]
    first = 0.9 * one_ref[...] + 0.1 * grad
    second = 0.999 * two_ref[...] + 0.001 * grad * grad
    first_ref[...] = first
    second_ref[...] = second
    new_ref[...] = gauss_ref[...] - 0.01 * first / (jnp.sqrt(second) + 1e-08)


def pin(value):
    return pltpu.with_memory_space_constraint(value, pltpu.HBM)


def body(gaussians, moment_one, moment_two, cameras, requests, tile_lists, tile_lengths, cotangent):
    vmem = pl.BlockSpec(memory_space=pltpu.VMEM)
    hbm = pl.BlockSpec(memory_space=pltpu.HBM)
    message = (N_TILE, 1, 128)
    plane = (PIX, SLOTS)
    back, own, one, two = pl.pallas_call(
        splat_kernel,
        out_shape=[pltpu.VMEM((N_CAM, 10, 1, OWN), f32)] + [pltpu.VMEM(gaussians.shape, f32)] * 3,
        in_specs=[hbm, hbm, hbm, hbm, pl.BlockSpec(memory_space=pltpu.SMEM), hbm, hbm, hbm],
        out_specs=[vmem] * 4,
        scratch_shapes=[
            pltpu.VMEM((1, 4), f32),
            pltpu.VMEM((1, SLOTS), jnp.int32),
            pltpu.VMEM((1, SLOTS), jnp.int32),
            pltpu.VMEM((3, 1, PIX), f32),
            pltpu.VMEM((8, 1, 128), jnp.int32),
            pltpu.VMEM(message, jnp.int32),
            pltpu.VMEM(message, f32),
            pltpu.VMEM(message, f32),
            pltpu.VMEM(message, f32),
            pltpu.VMEM(message, f32),
            pltpu.VMEM((10, 1, OWN), f32),
            pltpu.VMEM((128, SLOTS), bf16),
            pltpu.VMEM((3 * N_TILE, SLOTS), bf16),
            pltpu.VMEM(plane, f32),
            pltpu.VMEM(plane, f32),
            pltpu.VMEM(plane, f32),
            pltpu.VMEM(plane, bf16),
            pltpu.VMEM(plane, bf16),
            pltpu.VMEM(plane, f32),
            pltpu.VMEM(plane, bf16),
            pltpu.VMEM(plane, bf16),
            pltpu.VMEM(plane, bf16),
            pltpu.VMEM(plane, bf16),
            pltpu.VMEM(plane, f32),
            pltpu.VMEM(plane, f32),
            pltpu.VMEM((128, 128), jnp.int32),
            pltpu.VMEM((SLOTS, N_TILE), bf16),
            pltpu.VMEM((SLOTS, 128), bf16),
        ]
        + [pltpu.SemaphoreType.DMA] * 15,
        compiler_params=pltpu.CompilerParams(
            collective_id=0, has_side_effects=True, vmem_limit_bytes=40 * 1024 * 1024
        ),
        name="splat",
    )(
        pin(gaussians), pin(cameras), pin(requests), pin(tile_lists.reshape(1, SLOTS)),
        tile_lengths, pin(cotangent.reshape(3, 1, PIX)), pin(moment_one), pin(moment_two),
    )
    leaf = jax.ShapeDtypeStruct(gaussians.shape, f32)
    return pl.pallas_call(
        update_kernel,
        out_shape=(leaf, leaf, leaf, leaf),
        in_specs=[vmem] * 4,
        out_specs=(vmem, vmem, vmem, vmem),
        compiler_params=pltpu.CompilerParams(vmem_limit_bytes=32 * 1024 * 1024),
        name="update",
    )(own, one, two, back)


def solution(mesh):
    return jax.shard_map(
        body,
        mesh=mesh,
        in_specs=(
            P(None, "tile"),
            P(None, "tile"),
            P(None, "tile"),
            P("cam", None),
            P("cam", "tile"),
            P("cam", "tile", None),
            P("cam", "tile"),
            P("cam", "tile", None, None),
        ),
        out_specs=(P(None, "tile"), P(None, "tile"), P(None, "tile"), P(None, "tile")),
        check_vma=False,
    )
```

```python
import jax
import jax.numpy as jnp
from jax import lax
from jax.experimental import pallas as pl
from jax.experimental.pallas import tpu as pltpu
from jax.sharding import PartitionSpec as P

f32 = jnp.float32
bf16 = jnp.bfloat16
MESH = pl.DeviceIdType.MESH
N_TILE = 128
N_CAM = 4
OWN = 512
SLOTS = 1024
PIX = 256
GROUP = 256

focal_length = 350.0
dilation = 0.3
sh_zero = 0.28209479177387814
sh_one = 0.4886025119029199
sh_two = [
    1.0925484305920792,
    -1.0925484305920792,
    0.31539156525252005,
    -1.0925484305920792,
    0.5462742152960396,
]
sh_three = [
    -0.5900435899266435,
    2.890611442640554,
    -0.4570457994644658,
    0.3731763325901154,
    -0.4570457994644658,
    1.445305721320277,
    -0.5900435899266435,
]


def harmonics(dir_x, dir_y, dir_z):
    xx = dir_x * dir_x
    yy = dir_y * dir_y
    zz = dir_z * dir_z
    return [
        jnp.full_like(dir_x, sh_zero),
        -sh_one * dir_y,
        sh_one * dir_z,
        -sh_one * dir_x,
        sh_two[0] * dir_x * dir_y,
        sh_two[1] * dir_y * dir_z,
        sh_two[2] * (2.0 * zz - xx - yy),
        sh_two[3] * dir_x * dir_z,
        sh_two[4] * (xx - yy),
        sh_three[0] * dir_y * (3.0 * xx - yy),
        sh_three[1] * dir_x * dir_y * dir_z,
        sh_three[2] * dir_y * (4.0 * zz - xx - yy),
        sh_three[3] * dir_z * (2.0 * zz - 3.0 * xx - 3.0 * yy),
        sh_three[4] * dir_x * (4.0 * zz - xx - yy),
        sh_three[5] * dir_z * (xx - yy),
        sh_three[6] * dir_x * (xx - 3.0 * yy),
    ]


def screen_of(rows, camera, cos_yaw, sin_yaw):
    rel_x = rows[0] - camera[0]
    rel_y = rows[1] - camera[1]
    rel_z = rows[2] - camera[2]
    cam_x = cos_yaw * rel_x - sin_yaw * rel_z
    cam_z = sin_yaw * rel_x + cos_yaw * rel_z
    inv_depth = 1.0 / cam_z
    scaled = focal_length * inv_depth
    screen_x = scaled * cam_x + 128.0
    screen_y = scaled * rel_y + 64.0
    slant_x = -scaled * cam_x * inv_depth
    slant_y = -scaled * rel_y * inv_depth
    proj = [
        [scaled * cos_yaw + slant_x * sin_yaw, None, slant_x * cos_yaw - scaled * sin_yaw],
        [slant_y * sin_yaw, scaled, slant_y * cos_yaw],
    ]
    quat_norm = jnp.sqrt(
        rows[6] * rows[6] + rows[7] * rows[7] + rows[8] * rows[8] + rows[9] * rows[9]
    )
    inv_norm = 1.0 / quat_norm
    quat_w = rows[6] * inv_norm
    quat_x = rows[7] * inv_norm
    quat_y = rows[8] * inv_norm
    quat_z = rows[9] * inv_norm
    rotation = [
        [
            1.0 - 2.0 * (quat_y * quat_y + quat_z * quat_z),
            2.0 * (quat_x * quat_y - quat_w * quat_z),
            2.0 * (quat_x * quat_z + quat_w * quat_y),
        ],
        [
            2.0 * (quat_x * quat_y + quat_w * quat_z),
            1.0 - 2.0 * (quat_x * quat_x + quat_z * quat_z),
            2.0 * (quat_y * quat_z - quat_w * quat_x),
        ],
        [
            2.0 * (quat_x * quat_z - quat_w * quat_y),
            2.0 * (quat_y * quat_z + quat_w * quat_x),
            1.0 - 2.0 * (quat_x * quat_x + quat_y * quat_y),
        ],
    ]
    scales = [jnp.exp(rows[3]), jnp.exp(rows[4]), jnp.exp(rows[5])]
    shape_of = [[rotation[i][j] * scales[j] for j in range(3)] for i in range(3)]
    spread = [
        [proj[0][0] * shape_of[0][j] + proj[0][2] * shape_of[2][j] for j in range(3)],
        [
            proj[1][0] * shape_of[0][j] + proj[1][1] * shape_of[1][j] + proj[1][2] * shape_of[2][j]
            for j in range(3)
        ],
    ]
    cov_a = spread[0][0] ** 2 + spread[0][1] ** 2 + spread[0][2] ** 2 + dilation
    cov_b = spread[0][0] * spread[1][0] + spread[0][1] * spread[1][1] + spread[0][2] * spread[1][2]
    cov_c = spread[1][0] ** 2 + spread[1][1] ** 2 + spread[1][2] ** 2 + dilation
    inv_det = 1.0 / (cov_a * cov_c - cov_b * cov_b)
    inv_dist = 1.0 / jnp.sqrt(rel_x * rel_x + rel_y * rel_y + rel_z * rel_z)
    basis = harmonics(rel_x * inv_dist, rel_y * inv_dist, rel_z * inv_dist)
    colours = []
    for channel in range(3):
        acc_col = 0.5 + basis[0] * rows[11 + 16 * channel]
        for order in range(1, 16):
            acc_col = acc_col + basis[order] * rows[11 + 16 * channel + order]
        colours.append(acc_col)
    return [screen_x, screen_y, cov_c * inv_det, -cov_b * inv_det, cov_a * inv_det, *colours]


def parts_of(value, count):
    out = []
    for _ in range(count):
        part = value.astype(bf16).astype(f32)
        out.append(part)
        value = value - part
    return out


def dot(left, right, dims=((1,), (0,))):
    return lax.dot_general(left, right, (dims, ((), ())), preferred_element_type=f32)


def stack_rows(rows, count):
    width = rows[0].shape[1]
    at = lax.broadcasted_iota(jnp.int32, (count, width), 0)
    out = jnp.zeros((count, width), f32)
    for i, row in enumerate(rows):
        out = jnp.where(at == i, row, out)
    return out


def wait_for(ref, sem):
    pltpu.make_async_copy(ref, ref, sem).wait()


def splat_kernel(
    gauss_any, camera_any, req_any, list_any, length_any, cot_any, one_any, two_any,
    out_ref, gauss_ref, one_ref, two_ref,
    camera_ref, req_ref, list_ref, cot_ref,
    ask_out, ask_in, row_out, row_in, grad_out, grad_in, cam_out,
    picked, at_owner, gain, alpha, keep_a, keep_b, before, cot_wide,
    behind, wgain, turned, at_owner_t, picked_t,
    *sems,
):
    me = lax.axis_index("tile")
    cam = lax.axis_index("cam")
    high = me // 16
    low = lax.rem(me, 16)

    def peers(action):
        for step in (4, 3, 5, 2, 6, 1, 7, 0):
            row = jnp.bitwise_and(high + step, 7)
            for start, end in ((8, 16), (0, 8)) if step else ((8, 16), (1, 8)):

                @pl.loop(start, end)
                def _(i):
                    action(row * 16 + jnp.bitwise_and(low + i, 15), row)

    barrier = pltpu.get_barrier_semaphore()
    peers(
        lambda peer, row: pl.semaphore_signal(
            barrier, inc=1, device_id=(peer, cam), device_id_type=MESH
        )
    )
    for i in range(1, N_CAM):
        pl.semaphore_signal(
            barrier, inc=1, device_id=(me, lax.rem(cam + i, N_CAM)), device_id_type=MESH
        )
    loads = [
        pltpu.make_async_copy(src, dst, sem)
        for src, dst, sem in zip(
            (gauss_any, camera_any, req_any, list_any, cot_any, one_any, two_any),
            (gauss_ref, camera_ref, req_ref, list_ref, cot_ref, one_ref, two_ref),
            sems[8:15],
            strict=True,
        )
    ]
    for load in loads:
        load.start()

    def exchange(src, dst, send_sem, recv_sem, by_row=False):
        def send(peer, row):
            pltpu.make_async_remote_copy(
                src.at[row if by_row else peer], dst.at[me], send_sem, recv_sem,
                device_id=(peer, cam), device_id_type=MESH,
            ).start()

        peers(send)

    for load in loads[:5]:
        load.wait()
    for z in range(8):
        ask_out[z] = req_ref[:, 128 * z : 128 * (z + 1)]
    camera = camera_ref[...]
    heading = camera[:, 3:4]
    cos_yaw = jnp.cos(heading)
    sin_yaw = jnp.sin(heading)
    rows = [gauss_ref[i : i + 1, :] for i in range(59)]
    values = screen_of(
        rows, [camera[:, 0:1], camera[:, 1:2], camera[:, 2:3]], cos_yaw, sin_yaw
    )
    opacity = 1.0 / (1.0 + jnp.exp(-rows[10]))
    zero = jnp.zeros_like(opacity)
    table = stack_rows([*values[:5], opacity, zero, zero, *values[5:]], 16)
    table = jnp.concatenate(
        [part[:, 128 * c : 128 * (c + 1)] for part in parts_of(table, 3) for c in range(OWN // 128)],
        axis=0,
    ).astype(bf16)
    lane = lax.broadcasted_iota(jnp.int32, (1, OWN), 1)
    cam_row = jnp.zeros((1, OWN), f32)
    for i, value in enumerate(
        (camera[:, 0:1], camera[:, 1:2], camera[:, 2:3], cos_yaw, sin_yaw)
    ):
        cam_row = jnp.where(lane == i, value, cam_row)
    cam_out[9] = cam_row

    pl.semaphore_wait(barrier, N_TILE - 1 + N_CAM - 1)
    exchange(ask_out, ask_in, sems[0], sems[1], by_row=True)
    ask_in[me] = ask_out[high]

    list_row = list_ref[...]
    slot_owner = lax.shift_right_logical(list_row, 3)
    slot_part = jnp.bitwise_and(list_row, 7)
    of_owner = jnp.where(
        lax.broadcasted_iota(jnp.int32, (N_TILE, SLOTS), 0) == slot_owner, 1.0, 0.0
    )
    for i in range(3):
        at_owner[N_TILE * i : N_TILE * (i + 1), :] = of_owner.astype(bf16)
    live = (
        lax.broadcasted_iota(jnp.int32, (1, SLOTS), 1) < length_any[0, 0]
    )
    at_owner_t[...] = jnp.transpose(of_owner).astype(bf16)
    cot = stack_rows([cot_ref[0], cot_ref[1], cot_ref[2]], 8)
    cot_h, cot_m, cot_l = parts_of(cot, 3)
    wide = jnp.concatenate(
        [cot_h, cot_h, cot_h, cot_m, cot_m, cot_l, cot, jnp.zeros((72, PIX), f32)],
        axis=0,
    )
    wide = jnp.transpose(wide)
    for channel in range(3):
        cot_wide[channel] = jnp.broadcast_to(wide[:, 48 + channel : 49 + channel], (PIX, 128))
    wide = wide.astype(bf16)
    cot_cols = wide[:, 0:48]
    up = lax.broadcasted_iota(jnp.int32, (GROUP, GROUP), 0)
    down = lax.broadcasted_iota(jnp.int32, (GROUP, GROUP), 1)
    earlier = jnp.where(up < down, 1.0, 0.0).astype(bf16)
    later = jnp.where(up > down, 1.0, 0.0).astype(bf16)

    wait_for(ask_in.at[pl.ds(0, N_TILE - 1)], sems[1])

    asked = jnp.transpose(ask_in[:, 0, :])
    turned[...] = asked
    asked = turned[pl.ds(pl.multiple_of(low * 8, 8), 8), :]
    fine_at = lax.broadcasted_iota(jnp.int32, (128, 128), 0)
    coarse = lax.shift_right_logical(asked, 7)
    coarse = jnp.concatenate([coarse[s : s + 1] for s in range(8)], axis=1)
    asked = jnp.bitwise_and(asked, 127)
    for s in range(8):
        picked[:, 128 * s : 128 * (s + 1)] = jnp.where(
            fine_at == asked[s : s + 1, :], 1.0, 0.0
        ).astype(bf16)
    found = dot(table, picked[...])
    found = found[0:64] + found[64:128] + found[128:192]
    found = sum(
        jnp.where(coarse == c, found[16 * c : 16 * (c + 1)], 0.0) for c in range(OWN // 128)
    )
    found = jnp.concatenate([found[:, 128 * s : 128 * (s + 1)] for s in range(8)], axis=0)
    row_out[:, 0, :] = jnp.transpose(found)
    exchange(row_out, row_in, sems[2], sems[3])
    row_in[me] = row_out[me]
    picked_t[...] = jnp.transpose(picked[...].astype(f32)).astype(bf16)
    wait_for(row_in.at[pl.ds(0, N_TILE - 1)], sems[3])

    got = jnp.transpose(row_in[:, 0, :])
    got = jnp.concatenate(parts_of(got, 3), axis=1).astype(bf16)
    listed = dot(got, at_owner[...])
    slot = jnp.zeros((16, SLOTS), f32)
    for s in range(8):
        slot = slot + jnp.where(slot_part == s, listed[16 * s : 16 * (s + 1)], 0.0)
    tile_x = (lax.rem(me, 16) * 16 + 8).astype(f32)
    tile_y = (high * 16 + 8).astype(f32)
    off_x = slot[0:1] - tile_x
    off_y = slot[1:2] - tile_y
    con_a, con_b, con_c = slot[2:3], slot[3:4], slot[4:5]
    op_live = jnp.where(live, slot[5:6], 0.0)
    colour = parts_of(slot[8:16], 3)
    colour = jnp.concatenate(
        [colour[0], colour[1], colour[2], colour[0], colour[1], colour[0]], axis=0
    ).astype(bf16)
    gain[...] = dot(cot_cols, colour)

    groups = range(SLOTS // GROUP)
    line_x = lax.broadcasted_iota(jnp.int32, (16, GROUP), 0).astype(f32) - 7.5

    def blocks(group, step):
        step((slice(None), slice(GROUP * group, GROUP * (group + 1))))

    def split_to(value, ref_a, ref_b, at):
        part = value.astype(bf16)
        ref_a[at] = part
        ref_b[at] = (value - part.astype(f32)).astype(bf16)

    for g in groups:
        def opaque(at):
            cols = at[1]
            gap_x = line_x - off_x[:, cols]
            square = -0.5 * con_a[:, cols] * gap_x * gap_x
            cross = con_b[:, cols] * gap_x
            for y in range(16):
                gap_y = (y - 7.5) - off_y[:, cols]
                expo = square + (-0.5 * con_c[:, cols] * gap_y * gap_y - cross * gap_y)
                shade = op_live[:, cols] * jnp.exp(expo)
                line = (slice(16 * y, 16 * (y + 1)), cols)
                alpha[line] = shade
                split_to(jnp.log(1.0 - shade), keep_a, keep_b, line)

        blocks(g, opaque)

    def edge_of(inside, ref_a, ref_b, at):
        own = ref_a[:, at : at + 1].astype(f32) + ref_b[:, at : at + 1].astype(f32)
        edge = at % GROUP
        return jnp.broadcast_to(inside[:, edge : edge + 1] + own, (PIX, GROUP))

    carried = None
    for g in groups:
        cols = slice(GROUP * g, GROUP * (g + 1))
        inside = dot(keep_a[:, cols], earlier) + dot(keep_b[:, cols], earlier)
        if carried is not None:
            inside = inside + carried
        before[:, cols] = inside
        if g + 1 < len(groups):
            carried = edge_of(inside, keep_a, keep_b, GROUP * (g + 1) - 1)

    tints = [[], [], []]
    for g in groups:
        def weigh(at):
            sums = [None] * 3
            for y in range(16):
                line = (slice(16 * y, 16 * (y + 1)), at[1])
                weight = alpha[line] * jnp.exp(before[line])
                for channel in range(3):
                    column = cot_wide[channel, line[0], :]
                    term = jnp.concatenate([column, column], axis=1) * weight
                    sums[channel] = term if y == 0 else sums[channel] + term
                weighted = gain[line] * weight
                wgain[line] = weighted
                split_to(weighted, keep_a, keep_b, line)
            for channel in range(3):
                tints[channel].append(jnp.sum(sums[channel], axis=0, keepdims=True))

        blocks(g, weigh)

    carried = None
    for g in reversed(groups):
        cols = slice(GROUP * g, GROUP * (g + 1))
        inside = dot(keep_a[:, cols], later) + dot(keep_b[:, cols], later)
        if carried is not None:
            inside = inside + carried
        behind[:, cols] = inside
        if g:
            carried = edge_of(inside, keep_a, keep_b, GROUP * g)

    moments = [[] for _ in range(6)]
    for g in groups:
        def drop(at):
            plain = lifted = squared = None
            for y in range(16):
                line = (slice(16 * y, 16 * (y + 1)), at[1])
                shade = alpha[line]
                value = wgain[line] - behind[line] * (shade / (1.0 - shade))
                place = y - 7.5
                raised = place * value
                plain = value if y == 0 else plain + value
                lifted = raised if y == 0 else lifted + raised
                squared = place * raised if y == 0 else squared + place * raised
            pushed = line_x * plain
            for i, term in enumerate(
                (line_x * pushed, squared, line_x * lifted, pushed, lifted, plain)
            ):
                moments[i].append(jnp.sum(term, axis=0, keepdims=True))

        blocks(g, drop)

    tint = stack_rows([jnp.concatenate(parts, axis=1) for parts in tints], 8)
    m_xx, m_yy, m_xy, m_x, m_y, m_one = (jnp.concatenate(parts, axis=1) for parts in moments)
    m_du = m_x - off_x * m_one
    m_dv = m_y - off_y * m_one
    slot_grad = stack_rows(
        [
            con_a * m_du + con_b * m_dv,
            con_c * m_dv + con_b * m_du,
            -0.5 * (m_xx - off_x * (m_x + m_du)),
            -(m_xy - off_x * m_y - off_y * m_du),
            -0.5 * (m_yy - off_y * (m_y + m_dv)),
            m_one,
        ],
        8,
    )
    slot_grad = jnp.concatenate([slot_grad, tint], axis=0)

    spread = jnp.concatenate(
        [jnp.where(slot_part == s, slot_grad, 0.0) for s in range(8)], axis=0
    )
    spread = jnp.concatenate(parts_of(spread, 2), axis=0).astype(bf16)
    sums = dot(spread, at_owner_t[...])
    sums = jnp.transpose(sums[0:128] + sums[128:256])
    grad_out[:, 0, :] = sums
    exchange(grad_out, grad_in, sems[4], sems[5])
    grad_in[me] = grad_out[me]
    wait_for(grad_in.at[pl.ds(0, N_TILE - 1)], sems[5])

    back = jnp.transpose(grad_in[:, 0, :])
    back = jnp.concatenate([back[16 * s : 16 * (s + 1)] for s in range(8)], axis=1)
    back = jnp.concatenate(parts_of(back, 2), axis=0)
    back = jnp.concatenate(
        [jnp.where(coarse == c, back, 0.0) for c in range(OWN // 128)], axis=0
    ).astype(bf16)
    back = dot(back, picked_t[...])
    back = jnp.concatenate(
        [back[32 * c : 32 * c + 16] + back[32 * c + 16 : 32 * (c + 1)] for c in range(OWN // 128)],
        axis=1,
    )
    for i, at in enumerate((0, 1, 2, 3, 4, 5, 8, 9, 10)):
        cam_out[i] = back[at : at + 1]

    for i in range(1, N_CAM):
        pltpu.make_async_remote_copy(
            cam_out, out_ref.at[cam], sems[6], sems[7],
            device_id=(me, lax.rem(cam + i, N_CAM)), device_id_type=MESH,
        ).start()
    out_ref[cam] = cam_out[...]
    wait_for(out_ref.at[pl.ds(0, N_CAM - 1)], sems[7])
    wait_for(out_ref.at[pl.ds(0, N_CAM - 1)], sems[6])
    for load in loads[5:]:
        load.wait()
    for sem in (sems[0], sems[2], sems[4]):
        wait_for(row_in.at[pl.ds(0, N_TILE - 1)], sem)


def update_kernel(gauss_ref, one_ref, two_ref, back_ref, grad_ref, new_ref, first_ref, second_ref):
    half = OWN // 2
    first_half = lax.broadcasted_iota(jnp.int32, (8, half), 0) < N_CAM

    def spread(row):
        return jnp.where(first_half, row[:, :half], row[:, half:])

    def gathered(i):
        values = back_ref[:, i, 0, :]
        return jnp.concatenate([values[:, :half], values[:, half:]], axis=0)

    def over_cams(grad):
        return [jnp.sum(grad[at : at + N_CAM], axis=0, keepdims=True) for at in (0, N_CAM)]

    rows = [spread(gauss_ref[i : i + 1, :]) for i in range(59)]
    cam_rows = back_ref[:, 9, 0, 0:128]
    cam_rows = jnp.concatenate([cam_rows, cam_rows], axis=0)
    cams = [cam_rows[:, i : i + 1] for i in range(5)]

    def values_of(wanted):
        full = [*wanted[:10], None, *wanted[10:]]
        return screen_of(full, cams[:3], cams[3], cams[4])

    _, pull = jax.vjp(values_of, [*rows[:10], *rows[11:]])
    (grads,) = pull([gathered(i) for i in (0, 1, 2, 3, 4, 6, 7, 8)])
    shade = gathered(5) * (1.0 - 1.0 / (1.0 + jnp.exp(-rows[10])))
    for i, grad in enumerate([*grads[:10], shade, *grads[10:]]):
        low, high = over_cams(grad)
        grad_ref[i : i + 1, :half] = low
        grad_ref[i : i + 1, half:] = high
    grad = grad_ref[...]
    first = 0.9 * one_ref[...] + 0.1 * grad
    second = 0.999 * two_ref[...] + 0.001 * grad * grad
    first_ref[...] = first
    second_ref[...] = second
    new_ref[...] = gauss_ref[...] - 0.01 * first / (jnp.sqrt(second) + 1e-08)


def pin(value):
    return pltpu.with_memory_space_constraint(value, pltpu.HBM)


def body(gaussians, moment_one, moment_two, cameras, requests, tile_lists, tile_lengths, cotangent):
    vmem = pl.BlockSpec(memory_space=pltpu.VMEM)
    hbm = pl.BlockSpec(memory_space=pltpu.HBM)
    message = (N_TILE, 1, 128)
    plane = (PIX, SLOTS)
    back, own, one, two = pl.pallas_call(
        splat_kernel,
        out_shape=[pltpu.VMEM((N_CAM, 10, 1, OWN), f32)] + [pltpu.VMEM(gaussians.shape, f32)] * 3,
        in_specs=[hbm, hbm, hbm, hbm, pl.BlockSpec(memory_space=pltpu.SMEM), hbm, hbm, hbm],
        out_specs=[vmem] * 4,
        scratch_shapes=[
            pltpu.VMEM((1, 4), f32),
            pltpu.VMEM((1, SLOTS), jnp.int32),
            pltpu.VMEM((1, SLOTS), jnp.int32),
            pltpu.VMEM((3, 1, PIX), f32),
            pltpu.VMEM((8, 1, 128), jnp.int32),
            pltpu.VMEM(message, jnp.int32),
            pltpu.VMEM(message, f32),
            pltpu.VMEM(message, f32),
            pltpu.VMEM(message, f32),
            pltpu.VMEM(message, f32),
            pltpu.VMEM((10, 1, OWN), f32),
            pltpu.VMEM((128, SLOTS), bf16),
            pltpu.VMEM((3 * N_TILE, SLOTS), bf16),
            pltpu.VMEM(plane, f32),
            pltpu.VMEM(plane, f32),
            pltpu.VMEM(plane, bf16),
            pltpu.VMEM(plane, bf16),
            pltpu.VMEM(plane, f32),
            pltpu.VMEM((3, PIX, 128), f32),
            pltpu.VMEM(plane, f32),
            pltpu.VMEM(plane, f32),
            pltpu.VMEM((128, 128), jnp.int32),
            pltpu.VMEM((SLOTS, N_TILE), bf16),
            pltpu.VMEM((SLOTS, 128), bf16),
        ]
        + [pltpu.SemaphoreType.DMA] * 15,
        compiler_params=pltpu.CompilerParams(
            collective_id=0, has_side_effects=True, vmem_limit_bytes=40 * 1024 * 1024
        ),
        name="splat",
    )(
        pin(gaussians), pin(cameras), pin(requests), pin(tile_lists.reshape(1, SLOTS)),
        tile_lengths, pin(cotangent.reshape(3, 1, PIX)), pin(moment_one), pin(moment_two),
    )
    leaf = jax.ShapeDtypeStruct(gaussians.shape, f32)
    return pl.pallas_call(
        update_kernel,
        out_shape=(leaf, leaf, leaf, leaf),
        in_specs=[vmem] * 4,
        out_specs=(vmem, vmem, vmem, vmem),
        compiler_params=pltpu.CompilerParams(vmem_limit_bytes=32 * 1024 * 1024),
        name="update",
    )(own, one, two, back)


def solution(mesh):
    return jax.shard_map(
        body,
        mesh=mesh,
        in_specs=(
            P(None, "tile"),
            P(None, "tile"),
            P(None, "tile"),
            P("cam", None),
            P("cam", "tile"),
            P("cam", "tile", None),
            P("cam", "tile"),
            P("cam", "tile", None, None),
        ),
        out_specs=(P(None, "tile"), P(None, "tile"), P(None, "tile"), P(None, "tile")),
        check_vma=False,
    )
```
